32 devices in a mesh: section: 4 (over y, x), dp: 8 (over z, core).
Axes of the slice: x: 2, y: 2, z: 4, core: 2. Of those that a mesh axis runs over, the one named last changes fastest.
Arguments:
- inputs: bfloat16 [2, 5120, 512], P(None, 'dp'), may hold values from -6 to 6
- cotangent: bfloat16 [2, 5120, 512], P(None, 'dp'), may hold values from -6 to 6
- clip_lengths: int32 [2, 8, 4], P(None, 'dp'), may hold values from 0 to 640, as said below
- attention_gain: float32 [2, 512], replicated, may hold values from 0.5 to 1.5
- attention_bias: float32 [2, 512], replicated, may hold values from -3 to 3
- attention_in: bfloat16 [2, 512, 1536], replicated, may hold values from -0.25 to 0.25
- attention_out: bfloat16 [2, 512, 512], replicated, may hold values from -1 to 1
- feed_gain: float32 [2, 512], replicated, may hold values from 0.5 to 1.5
- feed_bias: float32 [2, 512], replicated, may hold values from -3 to 3
- feed_up: bfloat16 [2, 512, 2048], replicated, may hold values from -0.25 to 0.25
- feed_up_bias: float32 [2, 2048], replicated, may hold values from -3 to 3
- feed_down: bfloat16 [2, 2048, 512], replicated, may hold values from -0.125 to 0.125
- feed_down_bias: float32 [2, 512], replicated, may hold values from -3 to 3
Outputs:
- section_outputs: bfloat16 [4, 2, 5120, 512], P('section', None, 'dp')
- section_input_grads: bfloat16 [4, 2, 5120, 512], P('section', None, 'dp')
- grad_attention_gain: float32 [2, 512], replicated
- grad_attention_bias: float32 [2, 512], replicated
- grad_attention_in: float32 [2, 512, 1536], replicated
- grad_attention_out: float32 [2, 512, 512], replicated
- grad_feed_gain: float32 [2, 512], replicated
- grad_feed_bias: float32 [2, 512], replicated
- grad_feed_up: float32 [2, 512, 2048], replicated
- grad_feed_up_bias: float32 [2, 2048], replicated
- grad_feed_down: float32 [2, 2048, 512], replicated
- grad_feed_down_bias: float32 [2, 512], replicated
The draws below stay inside these ranges and needn't reach their ends.
Inputs may be any that keep to these rules, and one draw needn't show every extreme that they name: `clip_lengths`: each device's 4 lengths of a micro-batch sum to 640; a clip may be empty; in every micro-batch some device holds a single clip of all 640 tokens.
All inputs are finite; a program needn't handle non-finite values.
Results may differ from the reference program's by a relative error of at most 0.017.
Values may be sent and summed in bfloat16 or wider, within the bound.
A program may use at most 320 MiB of HBM per device.

```python
import jax
import jax.numpy as jnp
from jax import lax

D = 512
HEADS = 8
HEAD = 64
FF = 2048
LAYERS = 2
CLIPS = 4
MICRO = 2
TOK_DEV = 640
TOKENS = 5120
N_SECTION = 4
N_DP = 8


def draw_clip_lengths(key, part):
    key = jax.random.fold_in(key, 11)
    key_cuts, key_long, key_forced = jax.random.split(key, 3)
    cuts = jax.random.randint(key_cuts, (MICRO, N_DP, CLIPS - 1), 0, TOK_DEV + 1)
    cuts = jnp.sort(cuts, axis=-1)
    single = jax.random.randint(key_long, (MICRO, N_DP), 0, 84) < 16
    forced = jax.random.randint(key_forced, (MICRO,), 0, N_DP)
    single = single | (jnp.arange(N_DP)[None, :] == forced[:, None])
    cuts = jnp.where(single[..., None], TOK_DEV, cuts)
    edges = jnp.concatenate([jnp.zeros((MICRO, N_DP, 1), jnp.int32), cuts.astype(jnp.int32), jnp.full((MICRO, N_DP, 1), TOK_DEV, jnp.int32)], axis=-1)
    return (edges[..., 1:] - edges[..., :-1]).astype(jnp.int32)


def block_scale(stream_key, extent, cuts, least, largest):
    level, own = 1.0, jax.random.fold_in(stream_key, 6)
    for axis_at, parts in cuts:
        draws = jnp.exp(jax.random.uniform(jax.random.fold_in(own, axis_at), (parts,), jnp.float32, least / len(cuts), largest / len(cuts)))
        level = level * jnp.repeat(draws, extent[axis_at] // parts).reshape([-1 if axis == axis_at else 1 for axis in range(len(extent))])
    return level


def gaussian(stream_key, shape, deviation, bound, pieces=(), held_as=jnp.bfloat16):
    drawn = deviation * jax.random.normal(stream_key, shape, jnp.float32)
    if pieces:
        drawn = drawn * block_scale(stream_key, shape, pieces, -0.22, 0.18)
    return jnp.clip(drawn, -bound, bound).astype(held_as)


def setup_inputs(seed: int = 0) -> dict:
    seeds = jax.random.split(jax.random.key(seed), 14)
    inputs = gaussian(seeds[0], (MICRO, TOKENS, D), 1.0, 6.0, ((1, 8),))
    cotangent = gaussian(seeds[1], (MICRO, TOKENS, D), 1.0, 6.0, ((1, 8),))
    clip_lengths = draw_clip_lengths(jax.random.fold_in(seeds[13], 71), 0)
    attention_gain = jnp.clip(1.0 + 0.1 * jax.random.normal(seeds[3], (LAYERS, D), jnp.float32), 0.5, 1.5)
    attention_bias = gaussian(seeds[4], (LAYERS, D), 0.5, 3.0, (), jnp.float32)
    attention_in = gaussian(seeds[5], (LAYERS, D, 3 * D), D ** -0.5, 0.25)
    attention_out = gaussian(seeds[6], (LAYERS, D, D), (D // 16) ** -0.5, 1.0)
    feed_gain = jnp.clip(1.0 + 0.1 * jax.random.normal(seeds[7], (LAYERS, D), jnp.float32), 0.5, 1.5)
    feed_bias = gaussian(seeds[8], (LAYERS, D), 0.5, 3.0, (), jnp.float32)
    feed_up = gaussian(seeds[9], (LAYERS, D, FF), D ** -0.5, 0.25)
    feed_up_bias = gaussian(seeds[10], (LAYERS, FF), 0.5, 3.0, (), jnp.float32)
    feed_down = gaussian(seeds[11], (LAYERS, FF, D), FF ** -0.5, 0.125)
    feed_down_bias = gaussian(seeds[12], (LAYERS, D), 0.5, 3.0, (), jnp.float32)
    return dict(inputs=inputs, cotangent=cotangent, clip_lengths=clip_lengths, attention_gain=attention_gain, attention_bias=attention_bias, attention_in=attention_in, attention_out=attention_out, feed_gain=feed_gain, feed_bias=feed_bias, feed_up=feed_up, feed_up_bias=feed_up_bias, feed_down=feed_down, feed_down_bias=feed_down_bias)


@jax.custom_vjp
def low(v):
    return lax.optimization_barrier(v.astype(jnp.bfloat16)).astype(jnp.float32)

@jax.custom_vjp
def low_back(v):
    return v

def low_keep(v):
    return (low(v), None)

def low_pass(kept, grad):
    return (grad,)

def back_keep(v):
    return (v, None)

def back_low(kept, grad):
    return (low(grad),)
low.defvjp(low_keep, low_pass)
low_back.defvjp(back_keep, back_low)
EPS = 1e-05
TANH_SCALE = 0.7978845608028654
CUBIC = 0.044715
MASKED = -1e+30
HIGH = lax.Precision.HIGHEST

def matmul(left, right):
    return jnp.dot(left, right, precision=HIGH)

def layer_norm(hidden, gain, bias):
    mean = lax.optimization_barrier(jnp.mean(hidden, axis=-1, keepdims=True))
    centred = hidden - mean
    spread = lax.optimization_barrier(jnp.mean(centred * centred, axis=-1, keepdims=True))
    return centred * lax.rsqrt(spread + EPS) * gain + bias

def gelu(pre):
    return 0.5 * pre * (1.0 + jnp.tanh(TANH_SCALE * (pre + CUBIC * pre * pre * pre)))

def clip_mask(lengths):
    ends = jnp.cumsum(lengths)
    position = jnp.arange(TOK_DEV, dtype=jnp.int32)
    clip_of = lax.optimization_barrier(jnp.sum((position[:, None] >= ends[None, :-1]).astype(jnp.int32), axis=1))
    return (clip_of[:, None] == clip_of[None, :]) & (position[None, :] <= position[:, None])

def attention_branch(hidden, gain, bias, proj_in, proj_out, mask):
    normal = low(layer_norm(hidden, gain, bias))
    packed = low(low_back(matmul(normal, proj_in)))
    query = packed[:, :D].reshape(TOK_DEV, HEADS, HEAD)
    keys = packed[:, D:2 * D].reshape(TOK_DEV, HEADS, HEAD)
    values = packed[:, 2 * D:].reshape(TOK_DEV, HEADS, HEAD)
    scores = low_back(jnp.einsum('qhd,khd->hqk', query, keys, precision=HIGH) * HEAD ** (-0.5))
    scores = jnp.where(mask[None], scores, MASKED)
    top = lax.optimization_barrier(jnp.max(scores, axis=-1, keepdims=True))
    powers = jnp.exp(scores - top)
    probs = powers / lax.optimization_barrier(jnp.sum(powers, axis=-1, keepdims=True))
    mixed = jnp.einsum('hqk,khd->qhd', low(probs), values, precision=HIGH).reshape(TOK_DEV, D)
    mixed = low(low_back(mixed))
    return low_back(matmul(mixed, proj_out))

def feed_branch(hidden, gain, bias, up_proj, up_shift, down_proj, down_shift):
    normal = low(layer_norm(hidden, gain, bias))
    pre = low_back(matmul(normal, up_proj) + up_shift)
    inner = low(gelu(pre))
    return low_back(matmul(inner, down_proj) + down_shift)

def group_forward(block_in, probes, params, mask):
    a_gain, a_bias, a_in, a_out, f_gain, f_bias, f_up, f_up_bias, f_down, f_down_bias = params
    hidden = low_back(block_in + probes[0])
    outs = []
    total = hidden
    for section in range(N_SECTION):
        layer = section // 2
        if section % 2 == 0:
            branch = attention_branch(hidden, a_gain[layer], a_bias[layer], a_in[layer], a_out[layer], mask)
        else:
            branch = feed_branch(hidden, f_gain[layer], f_bias[layer], f_up[layer], f_up_bias[layer], f_down[layer], f_down_bias[layer])
        total = hidden + branch
        rounded = low(total)
        outs.append(rounded)
        if section + 1 < N_SECTION:
            hidden = low_back(rounded + probes[section + 1])
    return (total, jnp.stack(outs))

def reference(inputs, cotangent, clip_lengths, attention_gain, attention_bias, attention_in, attention_out, feed_gain, feed_bias, feed_up, feed_up_bias, feed_down, feed_down_bias):
    params = tuple((item.astype(jnp.float32) for item in (attention_gain, attention_bias, attention_in, attention_out, feed_gain, feed_bias, feed_up, feed_up_bias, feed_down, feed_down_bias)))
    groups = MICRO * N_DP
    block_in = inputs.astype(jnp.float32).reshape(groups, TOK_DEV, D)
    block_cot = cotangent.astype(jnp.float32).reshape(groups, TOK_DEV, D)
    block_len = clip_lengths.reshape(groups, CLIPS).astype(jnp.int32)

    def step(carry, item):
        rows_in, rows_cot, lengths = item
        mask = clip_mask(lengths)
        probes = jnp.zeros((N_SECTION, TOK_DEV, D), jnp.float32)
        total, pull, outs = jax.vjp(lambda probe, weights: group_forward(rows_in, probe, weights, mask), probes, params, has_aux=True)
        d_probes, d_params = pull(rows_cot)
        carry = jax.tree.map(jnp.add, carry, d_params)
        return (carry, (outs.astype(jnp.bfloat16), d_probes.astype(jnp.bfloat16)))
    start = tuple((jnp.zeros_like(item) for item in params))
    sums, (outs, d_probes) = lax.scan(step, start, (block_in, block_cot, block_len))

    def arrange(values):
        values = values.reshape(MICRO, N_DP, N_SECTION, TOK_DEV, D)
        return jnp.transpose(values, (2, 0, 1, 3, 4)).reshape(N_SECTION, MICRO, N_DP * TOK_DEV, D)
    return (arrange(outs), arrange(d_probes), sums[0], sums[1], sums[2], sums[3], sums[4], sums[5], sums[6], sums[7], sums[8], sums[9])
```

```python
import functools

import jax
import jax.numpy as jnp
from jax import lax
from jax.experimental import pallas as pl
from jax.experimental.pallas import tpu as pltpu
from jax.sharding import PartitionSpec as P

HEAD = 64
PAIR = 2 * HEAD
LANES = 128
EPS = 1e-05
TANH_SCALE = 0.7978845608028654
CUBIC = 0.044715
MASKED = -1e30
QBLOCK = 256
ROWS = 128
WIDEN_ROWS = 64
CHUNK = 512
PIECE = 512
F32 = jnp.float32
BF16 = jnp.bfloat16
MESH = pl.DeviceIdType.MESH


def dot(left, right):
    return jnp.dot(left, right, preferred_element_type=F32)


def dot_nt(left, right):
    return lax.dot_general(left, right, (((1,), (1,)), ((), ())), preferred_element_type=F32)


def each(count, size, body, init=0):
    def step(i, carry):
        return body(pl.ds(pl.multiple_of(i * size, size), size), carry)

    return lax.fori_loop(0, count // size, step, init, unroll=True)


def fold(x, op):
    return op(x.reshape(x.shape[0] // 8, 8, x.shape[1]), axis=0)


def spans(count):
    return [(a, min(a + QBLOCK, count)) for a in range(0, count, QBLOCK)]


def tiles(width):
    return [slice(a, a + LANES) for a in range(0, width, LANES)]


def lane_half(shape, half):
    lane = lax.broadcasted_iota(jnp.int32, shape, 1)
    return (lane < HEAD) if half == 0 else (lane >= HEAD)


def norm_forward(src, ones, gain, shift, stat, inv, xhat, normal):
    count, width = src.shape
    stat[0] = dot(src[...], ones[...]) * (1.0 / width)

    def first(rows, carry):
        mean = stat[0, rows, :]
        for cols in tiles(width):
            centred = src[rows, cols].astype(F32) - mean
            normal[rows, cols] = (centred * centred).astype(BF16)
        return carry

    each(count, 64, first)
    inv[...] = lax.rsqrt(dot(normal[...], ones[...]) * (1.0 / width) + EPS)

    def second(rows, carry):
        mean, scale = stat[0, rows, :], inv[rows, :]
        for cols in tiles(width):
            value = (src[rows, cols].astype(F32) - mean) * scale
            xhat[rows, cols] = value.astype(BF16)
            normal[rows, cols] = (value * gain[:, cols] + shift[:, cols]).astype(BF16)
        return carry

    each(count, 64, second)


def norm_again(xhat, gain, shift, normal):
    def body(rows, carry):
        normal[rows, :] = (xhat[rows, :].astype(F32) * gain + shift).astype(BF16)
        return carry

    each(xhat.shape[0], 32, body)


def norm_backward(xhat, inv, ones, gain, d_normal, up, low, low_product, stat, dst):
    count, width = xhat.shape

    def first(rows, carry):
        sums = list(carry)
        for i, cols in enumerate(tiles(width)):
            grad = d_normal[rows, cols]
            value = xhat[rows, cols].astype(F32)
            product = grad * value
            low[rows, cols] = (grad * gain[:, cols]).astype(BF16)
            low_product[rows, cols] = (product * gain[:, cols]).astype(BF16)
            sums[2 * i] += fold(product, jnp.sum)
            sums[2 * i + 1] += fold(grad, jnp.sum)
        return tuple(sums)

    sums = each(count, 64, first, (jnp.zeros((8, LANES), F32),) * (2 * width // LANES))
    stat[0] = dot(low[...], ones[...]) * (1.0 / width)
    stat[1] = dot(low_product[...], ones[...]) * (1.0 / width)

    def second(rows, carry):
        mean, inner, scale = stat[0, rows, :], stat[1, rows, :], inv[rows, :]
        for cols in tiles(width):
            value = xhat[rows, cols].astype(F32)
            back = scale * (d_normal[rows, cols] * gain[:, cols] - mean - value * inner)
            dst[rows, cols] = (up[rows, cols].astype(F32) + back).astype(BF16)
        return carry

    each(count, 64, second)
    total = [jnp.sum(part, axis=0, keepdims=True) for part in sums]
    return jnp.concatenate(total[0::2], axis=1), jnp.concatenate(total[1::2], axis=1)


def gelu_pair(pre):
    square = pre * pre
    tanh_value = jnp.tanh(pre * (TANH_SCALE + (TANH_SCALE * CUBIC) * square))
    half = 0.5 + 0.5 * tanh_value
    value = pre * half
    slope = half + value * (1.0 - tanh_value) * (
        TANH_SCALE + (3.0 * CUBIC * TANH_SCALE) * square
    )
    return value, slope


def build_mask(lengths, micro, bias):
    count = bias.shape[0]
    ends = [lengths[micro, 0]]
    for i in range(1, lengths.shape[1] - 1):
        ends.append(ends[-1] + lengths[micro, i])
    query = lax.broadcasted_iota(jnp.int32, (1, count), 1)
    start = jnp.zeros((1, count), jnp.int32)
    for end in ends:
        start = jnp.where(query >= end, end, start)

    def step(i, carry):
        rows = pl.ds(pl.multiple_of(i * ROWS, ROWS), ROWS)
        key = lax.broadcasted_iota(jnp.int32, (ROWS, count), 0) + i * ROWS
        bias[rows, :] = jnp.where((key >= start) & (key <= query), 0.0, MASKED).astype(BF16)
        return carry

    lax.fori_loop(0, count // ROWS, step, 0)


def attention_forward(in_here, out_here, src, norm, w_in, w_out, bias, normal, qkv, turned, probs, recip, scratch, mixed_t, dst):
    count, width = src.shape
    norm_forward(src, *norm, normal)
    in_here()
    for part in (1, 0, 2):
        cols = slice(part * width, (part + 1) * width)
        qkv[:, cols] = dot(normal[...], w_in[:, cols]).astype(BF16)
    turned[...] = jnp.transpose(qkv[:, 2 * width :])
    units = [(hp, half, a, b) for hp in range(width // PAIR) for a, b in spans(count) for half in range(2)]

    def scores(slot, unit):
        hp, half, a, b = unit
        lanes = slice(hp * PAIR, (hp + 1) * PAIR)
        query = qkv[a:b, lanes] * HEAD ** (-0.5)
        mine = jnp.where(lane_half(query.shape, half), query, 0).astype(BF16)
        scratch[slot, :b, : b - a] = dot_nt(qkv[:b, width + hp * PAIR : width + (hp + 1) * PAIR], mine)

    def finish(slot, unit):
        hp, half, a, b = unit
        span = b - a
        head = 2 * hp + half

        def first(rows, top):
            value = scratch[slot, rows, :span] + bias[rows, a:b].astype(F32)
            return jnp.maximum(top, fold(value, jnp.max))

        top = each(b, 64, first, jnp.full((8, span), MASKED, F32))
        top = jnp.max(top, axis=0, keepdims=True)

        def second(rows, summed):
            power = jnp.exp(scratch[slot, rows, :span] + bias[rows, a:b].astype(F32) - top)
            probs[head, rows, a:b] = power.astype(BF16)
            return summed + fold(power, jnp.sum)

        summed = each(b, 64, second, jnp.zeros((8, span), F32))
        scale = 1.0 / jnp.sum(summed, axis=0, keepdims=True)
        recip[head, :, a:b] = jnp.broadcast_to(scale, (8, span))
        rows = slice(head * HEAD, (head + 1) * HEAD)
        mixed_t[rows, a:b] = (dot(turned[rows, :b], probs[head, :b, a:b]) * scale).astype(BF16)

    for i, unit in enumerate(units):
        scores(i % 2, unit)
        if i:
            finish((i - 1) % 2, units[i - 1])
    finish((len(units) - 1) % 2, units[-1])
    out_here()
    branch = dot(jnp.transpose(mixed_t[...]), w_out[...])
    dst[...] = (src[...].astype(F32) + branch).astype(BF16)


def feed_forward(src, norm, w_up, b_up, w_down, b_down, normal, hidden, slope, scratch, total, dst):
    count, width = src.shape
    chunks = hidden.shape[1] // CHUNK
    norm_forward(src, *norm, normal)

    def finish(i):
        def body(rows, carry):
            cols = slice(i * CHUNK, (i + 1) * CHUNK)
            value, grade = gelu_pair(scratch[i % 2, rows, :] + b_up[:, cols])
            hidden[rows, cols] = value.astype(BF16)
            slope[rows, cols] = grade.astype(BF16)
            return carry

        each(count, 32, body)

    for i in range(chunks):
        scratch[i % 2] = dot(normal[...], w_up[:, i * CHUNK : (i + 1) * CHUNK])
        if i:
            finish(i - 1)
        if i == chunks - 1:
            total[...] = dot(hidden[:, : i * CHUNK], w_down[: i * CHUNK, :])
    finish(chunks - 1)
    done = (chunks - 1) * CHUNK
    branch = dot(hidden[:, done:], w_down[done:, :])
    dst[...] = (src[...].astype(F32) + b_down + total[...] + branch).astype(BF16)


def feed_backward(
    up, norm, w_up, w_down, normal, normal_t, hidden, slope, d_pre, other, scratch, total, dst, grads, vectors,
    side, tick, ready,
):
    count, width = up.shape
    ones, gain, shift, stat, inv, xhat = norm
    units = hidden.shape[1]
    mine = units // 2
    base = 2 * width
    norm_again(xhat, gain, shift, normal)
    normal_t[...] = jnp.transpose(normal[...])
    own = mine // CHUNK
    starts = [pl.multiple_of(side * mine, mine) + i * CHUNK for i in range(own)]
    starts += [pl.multiple_of((1 - side) * mine, mine) + i * CHUNK for i in range(own)]
    where = [pl.ds(pl.multiple_of(start, CHUNK), CHUNK) for start in starts]
    slots = d_pre.shape[1] // CHUNK
    place = [slice(i % slots * CHUNK, (i % slots + 1) * CHUNK) for i in range(2 * own)]

    def begin(i):
        scratch[i % 2] = dot_nt(up[...], w_down[where[i], :])

    def finish(i):
        def body(rows, summed):
            grad = (scratch[i % 2, rows, :] * slope[rows, where[i]].astype(F32)).astype(BF16)
            d_pre[rows, place[i]] = grad
            return summed + fold(grad.astype(F32), jnp.sum)

        summed = each(count, 32, body, jnp.zeros((8, CHUNK), F32))
        row = 5 + i % own + own * (side if i < own else 1 - side)
        vectors[pl.ds(row, 1), :] = jnp.sum(summed, axis=0, keepdims=True)

    def weights(i):
        grads[:, base + i * CHUNK : base + (i + 1) * CHUNK] = dot(normal_t[...], d_pre[:, place[i]]).astype(BF16)
        at = base + mine + i * width
        grads[:, at : at + width] = dot(jnp.transpose(hidden[:, where[i]]), up[...]).astype(BF16)

    begin(0)
    for i in range(1, 2 * own):
        begin(i)
        finish(i - 1)
        if i - 1 < own:
            weights(i - 1)
            tick(2.2)
            ready(base + (i - 1) * CHUNK, CHUNK)
            ready(base + mine + (i - 1) * width, width)
        else:
            tick(1.2)
        part = dot_nt(d_pre[:, place[i - 1]], w_up[:, where[i - 1]])
        total[...] = part if i == 1 else total[...] + part
    finish(2 * own - 1)
    total[...] += dot_nt(d_pre[:, place[2 * own - 1]], w_up[:, where[2 * own - 1]])
    vectors[4:5, :] = jnp.sum(each(count, 64, lambda rows, s: s + fold(up[rows, :].astype(F32), jnp.sum),
                                   jnp.zeros((8, width), F32)), axis=0, keepdims=True)
    tick(1.0)
    d_gain, d_bias = norm_backward(xhat, inv, ones, gain, total, up, normal, other, stat, dst)
    vectors[2:3, :] = d_gain
    vectors[3:4, :] = d_bias
    tick(1.0)


def feed_both(
    src, up, norm, w_up, b_up, w_down, b_down, normal, normal_t, hidden, d_pre, other, scratch, total, dst, back,
    grads, vectors, side, tick, ready, produced,
):
    count, width = src.shape
    ones, gain, shift, stat, inv, xhat = norm
    units = hidden.shape[1]
    mine = units // 2
    base = 2 * width
    own = mine // CHUNK
    norm_forward(src, *norm, normal)
    normal_t[...] = jnp.transpose(normal[...])
    starts = [pl.multiple_of(side * mine, mine) + i * CHUNK for i in range(own)]
    starts += [pl.multiple_of((1 - side) * mine, mine) + i * CHUNK for i in range(own)]
    where = [pl.ds(pl.multiple_of(start, CHUNK), CHUNK) for start in starts]
    slots = d_pre.shape[1] // CHUNK
    place = [slice(i % slots * CHUNK, (i % slots + 1) * CHUNK) for i in range(2 * own)]

    def begin(i):
        scratch[0] = dot(normal[...], w_up[:, where[i]])
        scratch[1] = dot_nt(up[...], w_down[where[i], :])

    def finish(i):
        offset = b_up[:, where[i]]

        def body(rows, summed):
            value, grade = gelu_pair(scratch[0, rows, :] + offset)
            hidden[rows, where[i]] = value.astype(BF16)
            grad = (scratch[1, rows, :] * grade).astype(BF16)
            d_pre[rows, place[i]] = grad
            return summed + fold(grad.astype(F32), jnp.sum)

        summed = each(count, 32, body, jnp.zeros((8, CHUNK), F32))
        row = 5 + i % own + own * (side if i < own else 1 - side)
        vectors[pl.ds(row, 1), :] = jnp.sum(summed, axis=0, keepdims=True)

    def weights(i):
        grads[:, base + i * CHUNK : base + (i + 1) * CHUNK] = dot(normal_t[...], d_pre[:, place[i]]).astype(BF16)
        at = base + mine + i * width
        grads[:, at : at + width] = dot(jnp.transpose(hidden[:, where[i]]), up[...]).astype(BF16)

    def through(i):
        part = dot_nt(d_pre[:, place[i]], w_up[:, where[i]])
        total[...] = part if i == 0 else total[...] + part

    begin(0)
    finish(0)
    for i in range(1, 2 * own):
        begin(i)
        if i - 1 < own:
            weights(i - 1)
        through(i - 1)
        finish(i)
        if i - 1 < own:
            tick(4.5 if i == 1 else 1.8)
            ready(base + (i - 1) * CHUNK, CHUNK)
            ready(base + mine + (i - 1) * width, width)
        else:
            tick(1.3)
    through(2 * own - 1)
    branch = dot(hidden[...], w_down[...])
    dst[...] = (src[...].astype(F32) + b_down + branch).astype(BF16)
    produced()
    vectors[4:5, :] = jnp.sum(each(count, 64, lambda rows, s: s + fold(up[rows, :].astype(F32), jnp.sum),
                                   jnp.zeros((8, width), F32)), axis=0, keepdims=True)
    tick(1.5)
    d_gain, d_bias = norm_backward(xhat, inv, ones, gain, total, up, normal, other, stat, back)
    vectors[2:3, :] = d_gain
    vectors[3:4, :] = d_bias
    tick(1.0)


def attention_backward(
    up, norm, w_in, w_out, normal, normal_t, qkv, turned, probs, recip, scratch, mixed_t, spread,
    d_mixed, d_scores, d_query_t, d_qkv, total, dst, grads, vectors, side, tick, ready,
):
    count, width = up.shape
    ones, gain, shift, stat, inv, xhat = norm
    quarter = width // 2
    third = 3 * quarter
    cols = pl.ds(pl.multiple_of(side * quarter, quarter), quarter)
    grads[:, third : third + quarter] = dot(mixed_t[...], up[:, cols]).astype(BF16)
    tick(0.5)
    ready(third, quarter)
    norm_again(xhat, gain, shift, normal)
    normal_t[...] = jnp.transpose(normal[...])
    scratch[0] = dot_nt(up[...], w_out[...])
    scratch[1] = lax.dot_general(
        recip[:, 0, :], spread[...], (((0,), (0,)), ((), ())), precision=lax.Precision.HIGHEST, preferred_element_type=F32
    )

    def scaled(rows, carry):
        d_mixed[rows, :] = (scratch[0, rows, :] * scratch[1, rows, :]).astype(BF16)
        return carry

    each(count, 32, scaled)
    turned[...] = jnp.transpose(qkv[:, width : 2 * width])
    scale = HEAD ** (-0.5)

    def pair(hp):
        lanes = pl.multiple_of(hp * PAIR, PAIR)
        values = qkv[:, pl.ds(pl.multiple_of(2 * width + lanes, PAIR), PAIR)]
        units = [(half, a, b) for a, b in spans(count) for half in range(2)]

        def begin(slot, unit):
            half, a, b = unit
            part = d_mixed[a:b, pl.ds(lanes, PAIR)]
            mine = jnp.where(lane_half(part.shape, half), part, 0).astype(BF16)
            scratch[slot, :b, : b - a] = dot_nt(values[:b], mine)

        def finish(slot, unit):
            half, a, b = unit
            span = b - a
            head = 2 * hp + half

            def first(rows, summed):
                return summed + fold(scratch[slot, rows, :span] * probs[head, rows, a:b].astype(F32), jnp.sum)

            inner = each(b, 64, first, jnp.zeros((8, span), F32))
            inner = jnp.sum(inner, axis=0, keepdims=True) * recip[head, 0:1, a:b]

            def second(rows, carry):
                prob = probs[head, rows, a:b].astype(F32)
                d_scores[half, rows, a:b] = (prob * (scratch[slot, rows, :span] - inner)).astype(BF16)
                return carry

            each(b, 64, second)
            rows = pl.ds(pl.multiple_of(lanes + half * HEAD, HEAD), HEAD)
            d_query_t[half * HEAD : (half + 1) * HEAD, a:b] = dot(turned[rows, :b], d_scores[half, :b, a:b])

        for i, unit in enumerate(units):
            begin(i % 2, unit)
            if i:
                finish((i - 1) % 2, units[i - 1])
        finish((len(units) - 1) % 2, units[-1])
        d_qkv[:, pl.ds(lanes, PAIR)] = (jnp.transpose(d_query_t[...]) * scale).astype(BF16)
        query = qkv[:, pl.ds(lanes, PAIR)] * scale
        part = d_mixed[:, pl.ds(lanes, PAIR)]
        masks = [lane_half((count, PAIR), half) for half in range(2)]
        queries = [jnp.where(mask, query, 0).astype(BF16) for mask in masks]
        parts = [jnp.where(mask, part, 0).astype(BF16) for mask in masks]
        for a, b in spans(count):
            d_key = sum(dot(d_scores[half, a:b, a:], queries[half][a:]) for half in range(2))
            d_value = sum(dot(probs[2 * hp + half, a:b, a:], parts[half][a:]) for half in range(2))
            d_qkv[a:b, pl.ds(pl.multiple_of(width + lanes, PAIR), PAIR)] = d_key.astype(BF16)
            d_qkv[a:b, pl.ds(pl.multiple_of(2 * width + lanes, PAIR), PAIR)] = d_value.astype(BF16)

    pairs = width // PAIR
    for i in range(pairs):
        pair((side * (pairs // 2) + i) % pairs)
        tick(2.0)
        if i == pairs // 2 - 1:
            for part in range(3):
                cols = pl.ds(pl.multiple_of(part * width + side * quarter, quarter), quarter)
                grads[:, part * quarter : (part + 1) * quarter] = dot(normal_t[...], d_qkv[:, cols]).astype(BF16)
            tick(0.8)
            ready(0, third)
    total[...] = dot_nt(d_qkv[...], w_in[...])
    tick(0.9)
    d_gain, d_bias = norm_backward(xhat, inv, ones, gain, total, up, normal, d_mixed, stat, dst)
    vectors[0:1, :] = d_gain
    vectors[1:2, :] = d_bias
    tick(1.0)


class Axis:
    def __init__(self, name, index, step):
        self.bit = (index // step) % 2
        self.device = {name: index + step * (1 - 2 * self.bit)}


class Request:
    def __init__(self, src, dst, name):
        self.src, self.dst, self.name, self.copy = src, dst, name, None
        self.size = jnp.dtype(src.dtype).itemsize
        for extent in src.shape:
            self.size *= extent


class Sums:
    RATE, CORE_RATE, LAG, AHEAD, STEP, MARGIN = 85e3, 150e3, 1.0, 8.0, 0.3, 1.0

    def __init__(self, grads, landed, gathered, vectors, landed_vectors, axes, side, sems):
        self.grads, self.landed, self.gathered = grads, landed, gathered
        self.vectors, self.landed_vectors = vectors, landed_vectors
        self.axes, self.side = axes, side
        self.send_sem, self.recv_sem, self.local_sem, self.free_sem = sems
        self.depth = [name for name in axes if name[0] == "z"]
        self.used = self.count = 0
        self.sent, self.locals, self.active, self.queue = [], [], [], []
        self.free, self.now = {}, 0.0

    def loads(self, name, size):
        if name == "core":
            return {"core": size / self.CORE_RATE}
        if name[0] != "z":
            return {name: 2 * size / self.RATE}
        loads = {"z": 2 * size / self.RATE}
        if name != "z0":
            loads["mid"] = (2 << int(name[1:])) * size / self.RATE
        return loads

    def occupy(self, name, size):
        for key, load in self.loads(name, size).items():
            self.free[key] = max(self.now, self.free.get(key, 0.0)) + load

    def issue(self, request):
        request.copy = pltpu.make_async_remote_copy(
            src_ref=request.src, dst_ref=request.dst,
            send_sem=self.send_sem.at[self.used], recv_sem=self.recv_sem.at[self.used],
            device_id=self.axes[request.name].device, device_id_type=MESH,
        )
        request.copy.start()
        self.used += 1
        self.sent.append(request.copy)
        self.occupy(request.name, request.size)
        return max(self.free[key] for key in self.loads(request.name, request.size)) + self.LAG

    def open_at(self, request):
        return max(self.free.get(key, 0.0) for key in self.loads(request.name, request.size)) - self.AHEAD

    def dispatch(self):
        for entry in sorted(self.queue, key=lambda entry: entry[:2]):
            if self.open_at(entry[2]) <= self.now:
                self.queue.remove(entry)
                group = entry[3]
                group["over"] = max(group["over"], self.issue(entry[2]))
                group["left"] -= 1
                if not group["left"]:
                    self.active.append((group["over"], entry[0], self.count, group["task"]))
                    self.count += 1

    def step(self, task, rank):
        requests = next(task, None)
        if requests is not None:
            group = {"left": len(requests), "over": 0.0, "task": task}
            for request in requests:
                self.queue.append((rank, self.count, request, group))
                self.count += 1

    def begin(self, task, rank):
        self.step(task, rank)
        self.dispatch()

    def tick(self, spent):
        self.now += spent
        stolen = 0.0
        self.dispatch()
        while self.active:
            entry = min(self.active, key=lambda entry: entry[:3])
            if entry[0] + self.MARGIN > self.now:
                break
            self.active.remove(entry)
            self.step(entry[3], entry[1])
            self.dispatch()
            stolen += self.STEP
        self.now += stolen

    def drain(self):
        while self.active or self.queue:
            self.dispatch()
            opens = min([self.open_at(entry[2]) for entry in self.queue], default=float("inf"))
            entry = min(self.active, key=lambda entry: entry[:3], default=None)
            if entry is None or self.now < opens < entry[0]:
                self.now = opens
                continue
            self.now = max(self.now, entry[0]) + self.STEP
            self.active.remove(entry)
            self.step(entry[3], entry[1])
        for copy in self.sent:
            copy.wait_send()
        for copy in self.locals:
            copy.wait()

    def done(self, copy):
        copy.wait_send()
        self.sent = [other for other in self.sent if other is not copy]

    def block(self, layer, start, size, order, after, task):
        cols = slice(start, start + size)
        here = lambda at, rows: self.grads.at[layer, pl.ds(pl.multiple_of(at, 16), rows), cols]
        at, rows, land, path = 0, self.grads.shape[1], 0, []
        half = rows // 2
        base = self.axes["core"].bit * half
        spare = lambda at, rows: self.landed.at[layer, pl.ds(pl.multiple_of(at, 16), rows), cols]
        there = lambda side: self.gathered.at[side, layer, pl.ds(pl.multiple_of(base, 16), half), cols]
        names = ["core"]
        for name in order:
            names += self.depth[1:] if name == "z1" else [name]
        for i, name in enumerate(names):
            bit = self.axes[name].bit
            last = i == len(names) - 1
            halve = not last and rows % 32 == 0
            keep = rows // 2 if halve else rows
            mine = at + bit * keep if halve else at
            away = at + (1 - bit) * keep if halve else at
            push = Request(here(away, keep), spare(land, keep), name)
            yield [push]
            push.copy.wait_recv()
            if not halve:
                self.done(push.copy)
            elif i:
                path.append((name, mine, keep))
            total = (here(mine, keep)[...].astype(F32) + spare(land, keep)[...].astype(F32)).astype(BF16)
            if last:
                spare(mine - base, keep)[...] = total
            else:
                here(mine, keep)[...] = total
            land += keep
            at, rows = mine, keep
        path = path[::-1]
        turn = len(path) - after
        for k, name in enumerate(["x"] + [step[0] for step in path[turn:]]):
            pl.semaphore_signal(
                self.free_sem.at[3 * task + k], inc=1, device_id=self.axes[name].device, device_id_type=MESH
            )
        at = at - base
        for name, mine, keep in path[:turn]:
            at = mine - base
            push = Request(spare(at, keep), spare(at, keep), name)
            yield [push]
            push.copy.wait_recv()
        if turn:
            at, rows = (path[turn][1] - base, path[turn][2]) if after else (0, half)

        def save(index, side):
            src = spare(index * half, half)
            copy = pltpu.make_async_copy(src, there(side), self.local_sem.at[2 * task + index])
            copy.start()
            self.locals.append(copy)
            return Request(src, there(side), "core")

        if not after:
            near = save(0, self.side)
        pl.semaphore_wait(self.free_sem.at[3 * task], 1)
        push = Request(spare(at, rows), spare(half + at, rows), "x")
        yield [push]
        push.copy.wait_recv()
        for k, (name, mine, keep) in enumerate(path[turn:]):
            pl.semaphore_wait(self.free_sem.at[3 * task + k + 1], 1)
            pushes = [Request(spare(at, keep), spare(at, keep), name) for at in (mine - base, half + mine - base)]
            yield pushes
            for push in pushes:
                push.copy.wait_recv()
        if after:
            near = save(0, self.side)
        far = save(1, 1 - self.side)
        yield [near, far]
        near.copy.wait_recv()
        far.copy.wait_recv()

    def vector(self, layer):
        for i, name in enumerate(["core", "y"] + self.depth):
            push = Request(self.vectors.at[layer], self.landed_vectors.at[layer, i], name)
            yield [push]
            push.copy.wait_recv()
            self.done(push.copy)
            self.vectors[layer] = self.vectors[layer] + self.landed_vectors[layer, i]


ORDERS = (
    (("y", "z0", "z1"), 1, 1),
    (("y", "z1", "z0"), 0, 2),
    (("z0", "z1", "y"), 0, 3),
    (("z0", "z1", "y"), 0, 4),
    (("z0", "y", "z1"), 0, 5),
    (("y", "z0", "z1"), 1, 6),
    (("y", "z1", "z0"), 0, 7),
    (("z0", "y", "z1"), 2, 8),
    (("z0", "z1", "y"), 0, 9),
    (("z0", "y", "z1"), 1, 10),
    (("y", "z1", "z0"), 1, 11),
    (("y", "z1", "z0"), 0, 12),
    (("z0", "y", "z1"), 0, 13),
    (("y", "z0", "z1"), 0, 14),
)


def chain_kernel(
    bits, lengths, a_gain, a_bias, f_gain, f_bias, b_up, b_down,
    inputs, cotangent, w_in_hbm, w_out_hbm, w_up_hbm, w_down_hbm,
    outs_hbm, backs_hbm, gathered, vectors, keep_probs, keep_hidden, keep_slope,
    w_in, w_out, w_up, w_down, states, backs, bias, ones, spread, stat, inv, xhat, normal, normal_t, qkv, turned,
    probs, recip, mixed_t, hidden, slope, total, scratch, wide, d_mixed, d_scores, d_query_t,
    grads, landed, landed_vectors,
    load_sem, save_sem, stash_sem, swap_send, swap_recv, sum_send, sum_recv, sum_local, sum_free,
):
    section = lax.axis_index("section")
    group = lax.axis_index("dp")
    micro = section // 2
    side = section % 2
    axes = {"x": Axis("section", section, 1), "y": Axis("section", section, 2), "core": Axis("dp", group, 1)}
    for i in range(bits):
        axes["z%d" % i] = Axis("dp", group, 2 << i)
    used = []

    def load(src, dst):
        copy = pltpu.make_async_copy(src, dst, load_sem.at[len(used)])
        copy.start()
        used.append(copy)
        return copy

    def load_attention(layer):
        return [load(w_in_hbm.at[layer], w_in), load(w_out_hbm.at[layer], w_out)]

    def load_feed(layer):
        return [load(w_up_hbm.at[layer], w_up), load(w_down_hbm.at[layer], w_down)]

    def wait(copies):
        for copy in copies:
            copy.wait()

    def stash(index, src, dst):
        copy = pltpu.make_async_copy(src, dst, stash_sem.at[index])
        copy.start()
        return copy

    first = [load(inputs.at[micro], states.at[0])]
    attention_loads = load_attention(0)

    barrier = pltpu.get_barrier_semaphore()
    for axis in axes.values():
        pl.semaphore_signal(barrier, inc=1, device_id=axis.device, device_id_type=MESH)
    build_mask(lengths, micro, bias)
    ones[...] = jnp.ones_like(ones)
    width = states.shape[2]
    row = lax.broadcasted_iota(jnp.int32, spread.shape, 0) * HEAD
    lane = lax.broadcasted_iota(jnp.int32, spread.shape, 1)
    spread[...] = jnp.where((lane >= row) & (lane < row + HEAD), 1.0, 0.0)
    vectors[...] = jnp.zeros_like(vectors)
    sums = Sums(grads, landed, gathered, vectors, landed_vectors, axes, side, (sum_send, sum_recv, sum_local, sum_free))
    partner = section + 2 - 4 * micro
    kept = []

    def swap(index, src, dst):
        return pltpu.make_async_remote_copy(
            src_ref=src.at[partner + 1 - index], dst_ref=dst.at[0, micro],
            send_sem=swap_send.at[index], recv_sem=swap_recv.at[index],
            device_id=axes["y"].device, device_id_type=MESH,
        )

    outward, inward = swap(0, states, outs_hbm), swap(1, backs, backs_hbm)

    def start_swap(copy, sublayer):
        @pl.when(partner == sublayer)
        def _():
            copy.start()

    def local(src, dst):
        copy = pltpu.make_async_copy(src, dst, save_sem.at[len(kept)])
        copy.start()
        kept.append(copy)

    def norm(sublayer):
        layer = sublayer // 2
        gain, shift = (a_gain, a_bias) if sublayer % 2 == 0 else (f_gain, f_bias)
        return (
            ones, gain[layer : layer + 1, :], shift[layer : layer + 1, :], stat, inv.at[sublayer], xhat.at[sublayer]
        )

    wait(first)
    saved = {}
    feed_loads, last = [], []

    def weights_here(layer):
        attention_loads[0].wait()
        if layer == 0:
            feed_loads.extend(load_feed(0))
            last.append(load(cotangent.at[micro], backs.at[4]))

    for layer in range(2):
        if layer == 1:
            saved["probs"].wait()
        attention_forward(
            functools.partial(weights_here, layer), attention_loads[1].wait,
            states.at[2 * layer], norm(2 * layer), w_in, w_out, bias, normal, qkv.at[layer], turned, probs,
            recip.at[layer], scratch, mixed_t.at[layer], states.at[2 * layer + 1],
        )
        if layer == 0:
            pl.semaphore_wait(barrier, len(axes))
        start_swap(outward, 2 * layer)
        if layer == 0:
            saved["probs"] = stash(0, probs, keep_probs)
            attention_loads = load_attention(1)
        wait(feed_loads)
        if layer == 1:
            break
        feed_forward(
            states.at[1], norm(1), w_up, b_up[:1, :], w_down, b_down[:1, :],
            normal, hidden, slope, scratch, total, states.at[2],
        )
        start_swap(outward, 1)
        saved["hidden"] = stash(1, hidden, keep_hidden)
        saved["slope"] = stash(2, slope, keep_slope)
        feed_loads = load_feed(1)
    swapped = 2 * states.shape[1] * width
    sums.now = 18.0
    sums.occupy("y", swapped // 2)
    sums.now = 22.0
    wait(last)
    saved["hidden"].wait()
    saved["slope"].wait()
    seen = []

    def ready(layer):
        def start(at, size):
            for first in range(at, at + size, PIECE):
                task = len(seen)
                order, after, rank = ORDERS[task % len(ORDERS)]
                sums.begin(sums.block(layer, first, min(PIECE, at + size - first), order, after, task), rank)
                seen.append(first)

        return start

    def produced():
        start_swap(outward, 3)
        local(states.at[section + 1], outs_hbm.at[0, micro])

    for layer in (1, 0):
        if layer == 1:
            feed_both(
                states.at[3], backs.at[4], norm(3), w_up, b_up.at[1:2, :], w_down, b_down[1:2, :],
                normal, normal_t, hidden, wide, d_mixed, scratch, total, states.at[4], backs.at[3],
                grads.at[1], vectors.at[1], side, sums.tick, ready(1), produced,
            )
        else:
            wait(feed_loads)
            saved["hidden"].wait()
            saved["slope"].wait()
            feed_backward(
                backs.at[2], norm(1), w_up, w_down, normal, normal_t, hidden, slope, wide,
                d_mixed, scratch, total, backs.at[1], grads.at[0], vectors.at[0], side, sums.tick, ready(0),
            )
        start_swap(inward, 2 * layer + 1)
        sums.occupy("y", swapped // 2 * layer)
        if layer == 1:
            saved["hidden"] = stash(3, keep_hidden, hidden)
            saved["slope"] = stash(4, keep_slope, slope)
            feed_loads = load_feed(0)
        else:
            wait(attention_loads)
            saved["probs"].wait()
        attention_backward(
            backs.at[2 * layer + 1], norm(2 * layer), w_in, w_out, normal, normal_t, qkv.at[layer], turned, probs,
            recip.at[layer], scratch, mixed_t.at[layer], spread, d_mixed, d_scores, d_query_t,
            wide.at[:, : qkv.shape[2]], total, backs.at[2 * layer], grads.at[layer], vectors.at[layer],
            side, sums.tick, ready(layer),
        )
        start_swap(inward, 2 * layer)
        sums.occupy("y", swapped // 2)
        sums.begin(sums.vector(layer), 0)
        if layer == 1:
            saved["probs"] = stash(5, keep_probs, probs)
            attention_loads = load_attention(0)
    local(backs.at[section], backs_hbm.at[0, micro])
    sums.drain()
    for copy in kept:
        copy.wait()
    outward.wait()
    inward.wait()


def run_chain(
    groups, inputs, cotangent, lengths, a_gain, a_bias, w_in, w_out, f_gain, f_bias, w_up, b_up, w_down, b_down
):
    _, count, width = inputs.shape
    layers, _, units = w_up.shape
    heads = width // HEAD
    bits = (groups // 2).bit_length() - 1
    vmem = pl.BlockSpec(memory_space=pltpu.VMEM)
    smem = pl.BlockSpec(memory_space=pltpu.SMEM)
    anywhere = pl.BlockSpec(memory_space=pl.ANY)
    shape = jax.ShapeDtypeStruct
    per_layer = 2 * width + units
    blocks = layers * (units // PIECE + 3)
    pushes = blocks * (3 * bits + 7) + layers * (bits + 2)
    return pl.pallas_call(
        functools.partial(chain_kernel, bits),
        out_shape=(
            shape((1, 2, count, width), BF16),
            shape((1, 2, count, width), BF16),
            shape((2, layers, width, per_layer), BF16),
            shape((layers, 16, width), F32),
            shape((heads, count, count), BF16),
            shape((count, units), BF16),
            shape((count, units), BF16),
        ),
        in_specs=[smem] + [vmem] * 6 + [anywhere] * 6,
        out_specs=[anywhere] * 3 + [vmem] + [anywhere] * 3,
        scratch_shapes=[
            pltpu.VMEM(w_in.shape[1:], BF16),
            pltpu.VMEM(w_out.shape[1:], BF16),
            pltpu.VMEM(w_up.shape[1:], BF16),
            pltpu.VMEM(w_down.shape[1:], BF16),
            pltpu.VMEM((2 * layers + 1, count, width), BF16),
            pltpu.VMEM((2 * layers + 1, count, width), BF16),
            pltpu.VMEM((count, count), BF16),
            pltpu.VMEM((width, LANES), BF16),
            pltpu.VMEM((heads, width), F32),
            pltpu.VMEM((2, count, LANES), F32),
            pltpu.VMEM((2 * layers, count, LANES), F32),
            pltpu.VMEM((2 * layers, count, width), BF16),
            pltpu.VMEM((count, width), BF16),
            pltpu.VMEM((width, count), BF16),
            pltpu.VMEM((layers, count, 3 * width), BF16),
            pltpu.VMEM((width, count), BF16),
            pltpu.VMEM((heads, count, count), BF16),
            pltpu.VMEM((layers, heads, 8, count), F32),
            pltpu.VMEM((layers, width, count), BF16),
            pltpu.VMEM((count, units), BF16),
            pltpu.VMEM((count, units), BF16),
            pltpu.VMEM((count, width), F32),
            pltpu.VMEM((2, count, CHUNK), F32),
            pltpu.VMEM((count, 3 * width), BF16),
            pltpu.VMEM((count, width), BF16),
            pltpu.VMEM((2, count, count), BF16),
            pltpu.VMEM((PAIR, count), F32),
            pltpu.VMEM((layers, width, per_layer), BF16),
            pltpu.VMEM((layers, width, per_layer), BF16),
            pltpu.VMEM((layers, bits + 2, 16, width), F32),
            pltpu.SemaphoreType.DMA((14,)),
            pltpu.SemaphoreType.DMA((2,)),
            pltpu.SemaphoreType.DMA((6,)),
            pltpu.SemaphoreType.DMA((2,)),
            pltpu.SemaphoreType.DMA((2,)),
            pltpu.SemaphoreType.DMA((pushes,)),
            pltpu.SemaphoreType.DMA((pushes,)),
            pltpu.SemaphoreType.DMA((2 * blocks,)),
            pltpu.SemaphoreType.REGULAR((3 * blocks,)),
        ],
        compiler_params=pltpu.CompilerParams(
            vmem_limit_bytes=63 * 1024 * 1024, collective_id=0, has_side_effects=True
        ),
        cost_estimate=pl.CostEstimate(
            flops=30_000_000_000, bytes_accessed=50_000_000, transcendentals=10_000_000
        ),
        name="chain",
    )(lengths[:, 0, :], a_gain, a_bias, f_gain, f_bias, b_up, b_down, inputs, cotangent, w_in, w_out, w_up, w_down)


def widen_kernel(
    block, vectors, outs_in, backs_in,
    g_in, g_out, g_up, g_down, a_gain, a_bias, f_gain, f_bias, b_up, b_down, outs, backs,
):
    width = g_out.shape[2]
    quarter = width // 2
    third = 3 * quarter
    units = g_up.shape[2] // 2
    parts = units // width
    first = (pl.program_id(0) == 0) & (pl.program_id(1) == 0)
    outs[...] = outs_in[...]
    backs[...] = backs_in[...]

    @pl.when(first)
    def _():
        for i, ref in enumerate([a_gain, a_bias, f_gain, f_bias, b_down]):
            ref[...] = vectors[:, i, :]
        for i in range(b_up.shape[1] // width):
            b_up[:, i * width : (i + 1) * width] = vectors[:, 5 + i, :]

    for side in range(2):
        for part in range(3):
            at = part * width + side * quarter
            g_in[0, :, at : at + quarter] = block[side, 0, :, part * quarter : (part + 1) * quarter].astype(F32)
        at = third
        g_out[0, :, side * quarter : (side + 1) * quarter] = block[side, 0, :, at : at + quarter].astype(F32)
        at += quarter
        g_up[0, :, side * units : (side + 1) * units] = block[side, 0, :, at : at + units].astype(F32)
        at += units
        for i in range(parts):
            g_down[0, side * parts + i] = block[side, 0, :, at + i * width : at + (i + 1) * width].astype(F32)


def widen(gathered, vectors, outs, backs):
    _, layers, width, cols = gathered.shape
    units = (cols - 2 * width) // 2
    parts = 2 * units // width
    shape = jax.ShapeDtypeStruct
    steps = width // WIDEN_ROWS
    stream = pl.BlockSpec((1, 1, outs.shape[2] // steps, width), lambda i, j: (0, i, j, 0))
    small = pl.BlockSpec((layers, width), lambda i, j: (0, 0))
    g_in, g_out, g_up, g_down, *rest = pl.pallas_call(
        widen_kernel,
        grid=(layers, steps),
        out_shape=(
            shape((layers, width, 3 * width), F32),
            shape((layers, width, width), F32),
            shape((layers, width, 2 * units), F32),
            shape((layers, parts, width, width), F32),
        )
        + (shape((layers, width), F32),) * 4
        + (shape((layers, 2 * units), F32), shape((layers, width), F32))
        + (shape(outs.shape, BF16), shape(backs.shape, BF16)),
        in_specs=[
            pl.BlockSpec((2, 1, WIDEN_ROWS, cols), lambda i, j: (0, i, j, 0)),
            pl.BlockSpec(vectors.shape, lambda i, j: (0, 0, 0)),
            stream,
            stream,
        ],
        out_specs=(
            pl.BlockSpec((1, WIDEN_ROWS, 3 * width), lambda i, j: (i, j, 0)),
            pl.BlockSpec((1, WIDEN_ROWS, width), lambda i, j: (i, j, 0)),
            pl.BlockSpec((1, WIDEN_ROWS, 2 * units), lambda i, j: (i, j, 0)),
            pl.BlockSpec((1, parts, WIDEN_ROWS, width), lambda i, j: (i, 0, j, 0)),
        )
        + (small,) * 4
        + (pl.BlockSpec((layers, 2 * units), lambda i, j: (0, 0)), small, stream, stream),
        compiler_params=pltpu.CompilerParams(vmem_limit_bytes=60 * 1024 * 1024),
        name="widen",
    )(gathered, vectors, outs, backs)
    return (g_in, g_out, g_up, g_down.reshape(layers, 2 * units, width), *rest)


def body(
    groups, inputs, cotangent, clip_lengths, attention_gain, attention_bias, attention_in, attention_out,
    feed_gain, feed_bias, feed_up, feed_up_bias, feed_down, feed_down_bias,
):
    outs, backs, gathered, vectors = run_chain(
        groups, inputs, cotangent, clip_lengths, attention_gain, attention_bias, attention_in, attention_out,
        feed_gain, feed_bias, feed_up, feed_up_bias, feed_down, feed_down_bias,
    )[:4]
    g_in, g_out, g_up, g_down, a_gain, a_bias, f_gain, f_bias, b_up, b_down, outs, backs = widen(
        gathered, vectors, outs, backs
    )
    return outs, backs, a_gain, a_bias, g_in, g_out, f_gain, f_bias, g_up, b_up, g_down, b_down


def solution(mesh):
    return jax.shard_map(
        functools.partial(body, mesh.shape["dp"]),
        mesh=mesh,
        in_specs=(P(None, "dp", None), P(None, "dp", None), P(None, "dp", None)) + (P(),) * 10,
        out_specs=(P("section", None, "dp", None), P("section", None, "dp", None)) + (P(),) * 10,
        check_vma=False,
    )
```

```python
import functools

import jax
import jax.numpy as jnp
from jax import lax
from jax.experimental import pallas as pl
from jax.experimental.pallas import tpu as pltpu
from jax.sharding import PartitionSpec as P

HEAD = 64
PAIR = 2 * HEAD
LANES = 128
EPS = 1e-05
TANH_SCALE = 0.7978845608028654
CUBIC = 0.044715
MASKED = -1e30
QBLOCK = 256
ROWS = 128
WIDEN_ROWS = 128
CHUNK = 512
PIECE = 512
F32 = jnp.float32
BF16 = jnp.bfloat16
MESH = pl.DeviceIdType.MESH


def dot(left, right):
    return jnp.dot(left, right, preferred_element_type=F32)


def dot_nt(left, right):
    return lax.dot_general(left, right, (((1,), (1,)), ((), ())), preferred_element_type=F32)


def each(count, size, body, init=0):
    def step(i, carry):
        return body(pl.ds(pl.multiple_of(i * size, size), size), carry)

    return lax.fori_loop(0, count // size, step, init, unroll=True)


def fold(x, op):
    return op(x.reshape(x.shape[0] // 8, 8, x.shape[1]), axis=0)


def spans(count):
    return [(a, min(a + QBLOCK, count)) for a in range(0, count, QBLOCK)]


def tiles(width):
    return [slice(a, a + LANES) for a in range(0, width, LANES)]


def lane_half(shape, half):
    lane = lax.broadcasted_iota(jnp.int32, shape, 1)
    return (lane < HEAD) if half == 0 else (lane >= HEAD)


def norm_forward(src, ones, gain, shift, stat, inv, xhat, normal):
    count, width = src.shape
    stat[0] = dot(src[...], ones[...]) * (1.0 / width)

    def first(rows, carry):
        mean = stat[0, rows, :]
        for cols in tiles(width):
            centred = src[rows, cols].astype(F32) - mean
            normal[rows, cols] = (centred * centred).astype(BF16)
        return carry

    each(count, 64, first)
    inv[...] = lax.rsqrt(dot(normal[...], ones[...]) * (1.0 / width) + EPS)

    def second(rows, carry):
        mean, scale = stat[0, rows, :], inv[rows, :]
        for cols in tiles(width):
            value = (src[rows, cols].astype(F32) - mean) * scale
            xhat[rows, cols] = value.astype(BF16)
            normal[rows, cols] = (value * gain[:, cols] + shift[:, cols]).astype(BF16)
        return carry

    each(count, 64, second)


def norm_again(xhat, gain, shift, normal):
    def body(rows, carry):
        normal[rows, :] = (xhat[rows, :].astype(F32) * gain + shift).astype(BF16)
        return carry

    each(xhat.shape[0], 32, body)


def norm_backward(xhat, inv, ones, gain, d_normal, up, low, low_product, stat, dst):
    count, width = xhat.shape

    def first(rows, carry):
        sums = list(carry)
        for i, cols in enumerate(tiles(width)):
            grad = d_normal[rows, cols]
            value = xhat[rows, cols].astype(F32)
            product = grad * value
            low[rows, cols] = (grad * gain[:, cols]).astype(BF16)
            low_product[rows, cols] = (product * gain[:, cols]).astype(BF16)
            sums[2 * i] += fold(product, jnp.sum)
            sums[2 * i + 1] += fold(grad, jnp.sum)
        return tuple(sums)

    sums = each(count, 64, first, (jnp.zeros((8, LANES), F32),) * (2 * width // LANES))
    stat[0] = dot(low[...], ones[...]) * (1.0 / width)
    stat[1] = dot(low_product[...], ones[...]) * (1.0 / width)

    def second(rows, carry):
        mean, inner, scale = stat[0, rows, :], stat[1, rows, :], inv[rows, :]
        for cols in tiles(width):
            value = xhat[rows, cols].astype(F32)
            back = scale * (d_normal[rows, cols] * gain[:, cols] - mean - value * inner)
            dst[rows, cols] = (up[rows, cols].astype(F32) + back).astype(BF16)
        return carry

    each(count, 64, second)
    total = [jnp.sum(part, axis=0, keepdims=True) for part in sums]
    return jnp.concatenate(total[0::2], axis=1), jnp.concatenate(total[1::2], axis=1)


def gelu_pair(pre):
    square = pre * pre
    tanh_value = jnp.tanh(pre * (TANH_SCALE + (TANH_SCALE * CUBIC) * square))
    half = 0.5 + 0.5 * tanh_value
    value = pre * half
    slope = half + value * (1.0 - tanh_value) * (
        TANH_SCALE + (3.0 * CUBIC * TANH_SCALE) * square
    )
    return value, slope


def gelu(pre):
    return pre * (0.5 + 0.5 * jnp.tanh(pre * (TANH_SCALE + (TANH_SCALE * CUBIC) * pre * pre)))


def build_mask(lengths, micro, bias):
    count = bias.shape[0]
    ends = [lengths[micro, 0]]
    for i in range(1, lengths.shape[1] - 1):
        ends.append(ends[-1] + lengths[micro, i])
    query = lax.broadcasted_iota(jnp.int32, (1, count), 1)
    start = jnp.zeros((1, count), jnp.int32)
    for end in ends:
        start = jnp.where(query >= end, end, start)

    def step(i, carry):
        rows = pl.ds(pl.multiple_of(i * ROWS, ROWS), ROWS)
        key = lax.broadcasted_iota(jnp.int32, (ROWS, count), 0) + i * ROWS
        bias[rows, :] = jnp.where((key >= start) & (key <= query), 0.0, MASKED)
        return carry

    lax.fori_loop(0, count // ROWS, step, 0)


def attention_forward(in_here, out_here, src, norm, w_in, w_out, bias, normal, qkv, turned, probs, recip, scratch, mixed_t, dst):
    count, width = src.shape
    norm_forward(src, *norm, normal)
    in_here()
    for part in (1, 0, 2):
        cols = slice(part * width, (part + 1) * width)
        qkv[:, cols] = dot(normal[...], w_in[:, cols]).astype(BF16)
    turned[...] = jnp.transpose(qkv[:, 2 * width :])
    units = [(hp, half, a, b) for hp in range(width // PAIR) for a, b in spans(count) for half in range(2)]

    def scores(slot, unit):
        hp, half, a, b = unit
        lanes = slice(hp * PAIR, (hp + 1) * PAIR)
        query = qkv[a:b, lanes] * HEAD ** (-0.5)
        mine = jnp.where(lane_half(query.shape, half), query, 0).astype(BF16)
        scratch[slot, :b, : b - a] = dot_nt(qkv[:b, width + hp * PAIR : width + (hp + 1) * PAIR], mine)

    def finish(slot, unit):
        hp, half, a, b = unit
        span = b - a
        head = 2 * hp + half

        def first(rows, top):
            value = scratch[slot, rows, :span] + bias[rows, a:b]
            return jnp.maximum(top, fold(value, jnp.max))

        top = each(b, 64, first, jnp.full((8, span), MASKED, F32))
        top = jnp.max(top, axis=0, keepdims=True)

        def second(rows, summed):
            power = jnp.exp(scratch[slot, rows, :span] + bias[rows, a:b] - top)
            probs[head, rows, a:b] = power.astype(BF16)
            return summed + fold(power, jnp.sum)

        summed = each(b, 64, second, jnp.zeros((8, span), F32))
        scale = 1.0 / jnp.sum(summed, axis=0, keepdims=True)
        recip[head, :, a:b] = jnp.broadcast_to(scale, (8, span))
        rows = slice(head * HEAD, (head + 1) * HEAD)
        mixed_t[rows, a:b] = (dot(turned[rows, :b], probs[head, :b, a:b]) * scale).astype(BF16)

    for i, unit in enumerate(units):
        scores(i % 2, unit)
        if i:
            finish((i - 1) % 2, units[i - 1])
    finish((len(units) - 1) % 2, units[-1])
    out_here()
    branch = dot(jnp.transpose(mixed_t[...]), w_out[...])
    dst[...] = (src[...].astype(F32) + branch).astype(BF16)


def feed_forward(src, norm, w_up, b_up, w_down, b_down, normal, hidden, scratch, total, dst):
    count, width = src.shape
    chunks = hidden.shape[1] // CHUNK
    norm_forward(src, *norm, normal)

    def finish(i):
        def body(rows, carry):
            cols = slice(i * CHUNK, (i + 1) * CHUNK)
            hidden[rows, cols] = gelu(scratch[i % 2, rows, :] + b_up[:, cols]).astype(BF16)
            return carry

        each(count, 32, body)

    for i in range(chunks):
        scratch[i % 2] = dot(normal[...], w_up[:, i * CHUNK : (i + 1) * CHUNK])
        if i:
            finish(i - 1)
        if i == chunks - 1:
            total[...] = dot(hidden[:, : i * CHUNK], w_down[: i * CHUNK, :])
    finish(chunks - 1)
    done = (chunks - 1) * CHUNK
    branch = dot(hidden[:, done:], w_down[done:, :])
    dst[...] = (src[...].astype(F32) + b_down + total[...] + branch).astype(BF16)


def feed_both(
    src, up, norm, w_up, b_up, w_down, b_down, normal, normal_t, hidden, d_pre, other, scratch, total, dst, back,
    grads, vectors, side, tick, ready, produced,
):
    count, width = src.shape
    ones, gain, shift, stat, inv, xhat = norm
    units = hidden.shape[1]
    mine = units // 2
    base = 2 * width
    own = mine // CHUNK
    if produced is None:
        norm_again(xhat, gain, shift, normal)
    else:
        norm_forward(src, *norm, normal)
    normal_t[...] = jnp.transpose(normal[...])
    starts = [pl.multiple_of(side * mine, mine) + i * CHUNK for i in range(own)]
    starts += [pl.multiple_of((1 - side) * mine, mine) + i * CHUNK for i in range(own)]
    where = [pl.ds(pl.multiple_of(start, CHUNK), CHUNK) for start in starts]
    slots = d_pre.shape[1] // CHUNK
    place = [slice(i % slots * CHUNK, (i % slots + 1) * CHUNK) for i in range(2 * own)]

    def begin(i):
        scratch[0] = dot(normal[...], w_up[:, where[i]])
        scratch[1] = dot_nt(up[...], w_down[where[i], :])

    def finish(i):
        offset = b_up[:, where[i]]

        def body(rows, summed):
            value, grade = gelu_pair(scratch[0, rows, :] + offset)
            hidden[rows, where[i]] = value.astype(BF16)
            grad = (scratch[1, rows, :] * grade).astype(BF16)
            d_pre[rows, place[i]] = grad
            return summed + fold(grad.astype(F32), jnp.sum)

        summed = each(count, 32, body, jnp.zeros((8, CHUNK), F32))
        row = 5 + i % own + own * (side if i < own else 1 - side)
        vectors[pl.ds(row, 1), :] = jnp.sum(summed, axis=0, keepdims=True)

    def weights(i):
        grads[:, base + i * CHUNK : base + (i + 1) * CHUNK] = dot(normal_t[...], d_pre[:, place[i]]).astype(BF16)
        at = base + mine + i * width
        grads[:, at : at + width] = dot(jnp.transpose(hidden[:, where[i]]), up[...]).astype(BF16)

    def through(i):
        part = dot_nt(d_pre[:, place[i]], w_up[:, where[i]])
        total[...] = part if i == 0 else total[...] + part

    def send(i):
        ready(base + i * CHUNK, CHUNK)
        ready(base + mine + i * width, width)

    begin(0)
    finish(0)
    weights(0)
    tick(3.2)
    send(0)
    for i in range(1, 2 * own):
        begin(i)
        through(i - 1)
        finish(i)
        if i < own:
            weights(i)
            tick(2.2)
            send(i)
        else:
            tick(1.5)
    through(2 * own - 1)
    if produced is not None:
        branch = dot(hidden[...], w_down[...])
        dst[...] = (src[...].astype(F32) + b_down + branch).astype(BF16)
        produced()
    vectors[4:5, :] = jnp.sum(each(count, 64, lambda rows, s: s + fold(up[rows, :].astype(F32), jnp.sum),
                                   jnp.zeros((8, width), F32)), axis=0, keepdims=True)
    tick(1.5)
    d_gain, d_bias = norm_backward(xhat, inv, ones, gain, total, up, normal, other, stat, back)
    vectors[2:3, :] = d_gain
    vectors[3:4, :] = d_bias
    tick(1.0)


def attention_backward(
    up, norm, w_in, w_out, normal, normal_t, qkv, turned, probs, recip, scratch, mixed_t, spread,
    d_mixed, d_scores, d_query_t, d_qkv, total, dst, grads, vectors, side, tick, ready,
):
    count, width = up.shape
    ones, gain, shift, stat, inv, xhat = norm
    quarter = width // 2
    third = 3 * quarter
    cols = pl.ds(pl.multiple_of(side * quarter, quarter), quarter)
    grads[:, third : third + quarter] = dot(mixed_t[...], up[:, cols]).astype(BF16)
    tick(0.5)
    ready(third, quarter)
    norm_again(xhat, gain, shift, normal)
    normal_t[...] = jnp.transpose(normal[...])
    scratch[0] = dot_nt(up[...], w_out[...])
    scratch[1] = lax.dot_general(
        recip[:, 0, :], spread[...], (((0,), (0,)), ((), ())), precision=lax.Precision.HIGHEST, preferred_element_type=F32
    )

    def scaled(rows, carry):
        d_mixed[rows, :] = (scratch[0, rows, :] * scratch[1, rows, :]).astype(BF16)
        return carry

    each(count, 32, scaled)
    turned[...] = jnp.transpose(qkv[:, width : 2 * width])
    scale = HEAD ** (-0.5)

    def pair(hp):
        lanes = pl.multiple_of(hp * PAIR, PAIR)
        values = qkv[:, pl.ds(pl.multiple_of(2 * width + lanes, PAIR), PAIR)]
        units = [(half, a, b) for a, b in spans(count) for half in range(2)]

        def begin(slot, unit):
            half, a, b = unit
            part = d_mixed[a:b, pl.ds(lanes, PAIR)]
            mine = jnp.where(lane_half(part.shape, half), part, 0).astype(BF16)
            scratch[slot, :b, : b - a] = dot_nt(values[:b], mine)

        def finish(slot, unit):
            half, a, b = unit
            span = b - a
            head = 2 * hp + half

            def first(rows, summed):
                return summed + fold(scratch[slot, rows, :span] * probs[head, rows, a:b].astype(F32), jnp.sum)

            inner = each(b, 64, first, jnp.zeros((8, span), F32))
            inner = jnp.sum(inner, axis=0, keepdims=True) * recip[head, 0:1, a:b]

            def second(rows, carry):
                prob = probs[head, rows, a:b].astype(F32)
                d_scores[half, rows, a:b] = (prob * (scratch[slot, rows, :span] - inner)).astype(BF16)
                return carry

            each(b, 64, second)
            rows = pl.ds(pl.multiple_of(lanes + half * HEAD, HEAD), HEAD)
            d_query_t[half * HEAD : (half + 1) * HEAD, a:b] = dot(turned[rows, :b], d_scores[half, :b, a:b])

        for i, unit in enumerate(units):
            begin(i % 2, unit)
            if i:
                finish((i - 1) % 2, units[i - 1])
        finish((len(units) - 1) % 2, units[-1])
        d_qkv[:, pl.ds(lanes, PAIR)] = (jnp.transpose(d_query_t[...]) * scale).astype(BF16)
        query = qkv[:, pl.ds(lanes, PAIR)] * scale
        part = d_mixed[:, pl.ds(lanes, PAIR)]
        masks = [lane_half((count, PAIR), half) for half in range(2)]
        queries = [jnp.where(mask, query, 0).astype(BF16) for mask in masks]
        parts = [jnp.where(mask, part, 0).astype(BF16) for mask in masks]
        for a, b in spans(count):
            d_key = sum(dot(d_scores[half, a:b, a:], queries[half][a:]) for half in range(2))
            d_value = sum(dot(probs[2 * hp + half, a:b, a:], parts[half][a:]) for half in range(2))
            d_qkv[a:b, pl.ds(pl.multiple_of(width + lanes, PAIR), PAIR)] = d_key.astype(BF16)
            d_qkv[a:b, pl.ds(pl.multiple_of(2 * width + lanes, PAIR), PAIR)] = d_value.astype(BF16)

    pairs = width // PAIR
    for i in range(pairs):
        pair((side * (pairs // 2) + i) % pairs)
        tick(2.0)
        if i == pairs // 2 - 1:
            for part in range(3):
                cols = pl.ds(pl.multiple_of(part * width + side * quarter, quarter), quarter)
                grads[:, part * quarter : (part + 1) * quarter] = dot(normal_t[...], d_qkv[:, cols]).astype(BF16)
            tick(0.8)
            ready(0, third)
    total[...] = dot_nt(d_qkv[...], w_in[...])
    tick(0.9)
    d_gain, d_bias = norm_backward(xhat, inv, ones, gain, total, up, normal, d_mixed, stat, dst)
    vectors[0:1, :] = d_gain
    vectors[1:2, :] = d_bias
    tick(1.0)


class Axis:
    def __init__(self, name, index, step):
        self.bit = (index // step) % 2
        self.device = {name: index + step * (1 - 2 * self.bit)}


class Request:
    def __init__(self, src, dst, name):
        self.src, self.dst, self.name, self.copy = src, dst, name, None
        self.size = jnp.dtype(src.dtype).itemsize
        for extent in src.shape:
            self.size *= extent


class Sums:
    RATE, CORE_RATE, LAG, AHEAD, STEP, MARGIN = 85e3, 150e3, 1.0, 8.0, 0.3, 1.0

    def __init__(self, grads, landed, gathered, vectors, landed_vectors, axes, side, sems):
        self.grads, self.landed, self.gathered = grads, landed, gathered
        self.vectors, self.landed_vectors = vectors, landed_vectors
        self.axes, self.side = axes, side
        self.send_sem, self.recv_sem, self.local_sem, self.free_sem = sems
        self.depth = [name for name in axes if name[0] == "z"]
        self.used = self.count = 0
        self.sent, self.locals, self.active, self.queue = [], [], [], []
        self.free, self.now = {}, 0.0

    def loads(self, name, size):
        if name == "core":
            return {"core": size / self.CORE_RATE}
        if name[0] != "z":
            return {name: 2 * size / self.RATE}
        loads = {"z": 2 * size / self.RATE}
        if name != "z0":
            loads["mid"] = (2 << int(name[1:])) * size / self.RATE
        return loads

    def occupy(self, name, size):
        for key, load in self.loads(name, size).items():
            self.free[key] = max(self.now, self.free.get(key, 0.0)) + load

    def issue(self, request):
        request.copy = pltpu.make_async_remote_copy(
            src_ref=request.src, dst_ref=request.dst,
            send_sem=self.send_sem.at[self.used], recv_sem=self.recv_sem.at[self.used],
            device_id=self.axes[request.name].device, device_id_type=MESH,
        )
        request.copy.start()
        self.used += 1
        self.sent.append(request.copy)
        self.occupy(request.name, request.size)
        return max(self.free[key] for key in self.loads(request.name, request.size)) + self.LAG

    def open_at(self, request):
        return max(self.free.get(key, 0.0) for key in self.loads(request.name, request.size)) - self.AHEAD

    def dispatch(self):
        for entry in sorted(self.queue, key=lambda entry: entry[:2]):
            if self.open_at(entry[2]) <= self.now:
                self.queue.remove(entry)
                group = entry[3]
                group["over"] = max(group["over"], self.issue(entry[2]))
                group["left"] -= 1
                if not group["left"]:
                    self.active.append((group["over"], entry[0], self.count, group["task"]))
                    self.count += 1

    def step(self, task, rank):
        requests = next(task, None)
        if requests is not None:
            group = {"left": len(requests), "over": 0.0, "task": task}
            for request in requests:
                self.queue.append((rank, self.count, request, group))
                self.count += 1

    def begin(self, task, rank):
        self.step(task, rank)
        self.dispatch()

    def tick(self, spent):
        self.now += spent
        stolen = 0.0
        self.dispatch()
        while self.active:
            entry = min(self.active, key=lambda entry: entry[:3])
            if entry[0] + self.MARGIN > self.now:
                break
            self.active.remove(entry)
            self.step(entry[3], entry[1])
            self.dispatch()
            stolen += self.STEP
        self.now += stolen

    def drain(self):
        while self.active or self.queue:
            self.dispatch()
            opens = min([self.open_at(entry[2]) for entry in self.queue], default=float("inf"))
            entry = min(self.active, key=lambda entry: entry[:3], default=None)
            if entry is None or self.now < opens < entry[0]:
                self.now = opens
                continue
            self.now = max(self.now, entry[0]) + self.STEP
            self.active.remove(entry)
            self.step(entry[3], entry[1])
        for copy in self.sent:
            copy.wait_send()
        for copy in self.locals:
            copy.wait()

    def done(self, copy):
        copy.wait_send()
        self.sent = [other for other in self.sent if other is not copy]

    def block(self, layer, start, size, order, after, task):
        cols = slice(start, start + size)
        here = lambda at, rows: self.grads.at[layer, pl.ds(pl.multiple_of(at, 16), rows), cols]
        at, rows, land, path = 0, self.grads.shape[1], 0, []
        half = rows // 2
        base = self.axes["core"].bit * half
        spare = lambda at, rows: self.landed.at[layer, pl.ds(pl.multiple_of(at, 16), rows), cols]
        there = lambda side: self.gathered.at[side, layer, pl.ds(pl.multiple_of(base, 16), half), cols]
        names = ["core"]
        for name in order:
            names += self.depth[1:] if name == "z1" else [name]
        for i, name in enumerate(names):
            bit = self.axes[name].bit
            last = i == len(names) - 1
            halve = not last and rows % 32 == 0
            keep = rows // 2 if halve else rows
            mine = at + bit * keep if halve else at
            away = at + (1 - bit) * keep if halve else at
            push = Request(here(away, keep), spare(land, keep), name)
            yield [push]
            push.copy.wait_recv()
            if not halve:
                self.done(push.copy)
            elif i:
                path.append((name, mine, keep))
            total = (here(mine, keep)[...].astype(F32) + spare(land, keep)[...].astype(F32)).astype(BF16)
            if last:
                spare(mine - base, keep)[...] = total
            else:
                here(mine, keep)[...] = total
            land += keep
            at, rows = mine, keep
        path = path[::-1]
        turn = len(path) - after
        for k, name in enumerate(["x"] + [step[0] for step in path[turn:]]):
            pl.semaphore_signal(
                self.free_sem.at[3 * task + k], inc=1, device_id=self.axes[name].device, device_id_type=MESH
            )
        at = at - base
        for name, mine, keep in path[:turn]:
            at = mine - base
            push = Request(spare(at, keep), spare(at, keep), name)
            yield [push]
            push.copy.wait_recv()
        if turn:
            at, rows = (path[turn][1] - base, path[turn][2]) if after else (0, half)

        def save(index, side):
            src = spare(index * half, half)
            copy = pltpu.make_async_copy(src, there(side), self.local_sem.at[2 * task + index])
            copy.start()
            self.locals.append(copy)
            return Request(src, there(side), "core")

        if not after:
            near = save(0, self.side)
        pl.semaphore_wait(self.free_sem.at[3 * task], 1)
        push = Request(spare(at, rows), spare(half + at, rows), "x")
        yield [push]
        push.copy.wait_recv()
        for k, (name, mine, keep) in enumerate(path[turn:]):
            pl.semaphore_wait(self.free_sem.at[3 * task + k + 1], 1)
            pushes = [Request(spare(at, keep), spare(at, keep), name) for at in (mine - base, half + mine - base)]
            yield pushes
            for push in pushes:
                push.copy.wait_recv()
        if after:
            near = save(0, self.side)
        far = save(1, 1 - self.side)
        yield [near, far]
        near.copy.wait_recv()
        far.copy.wait_recv()

    def vector(self, layer):
        for i, name in enumerate(["core", "y"] + self.depth):
            push = Request(self.vectors.at[layer], self.landed_vectors.at[layer, i], name)
            yield [push]
            push.copy.wait_recv()
            self.done(push.copy)
            self.vectors[layer] = self.vectors[layer] + self.landed_vectors[layer, i]


ORDERS = (
    (("y", "z0", "z1"), 1, 1),
    (("y", "z1", "z0"), 0, 2),
    (("z0", "z1", "y"), 0, 3),
    (("z0", "z1", "y"), 0, 4),
    (("z0", "y", "z1"), 0, 5),
    (("y", "z0", "z1"), 1, 6),
    (("y", "z1", "z0"), 0, 7),
    (("z0", "y", "z1"), 2, 8),
    (("z0", "z1", "y"), 0, 9),
    (("z0", "y", "z1"), 1, 10),
    (("y", "z1", "z0"), 1, 11),
    (("y", "z1", "z0"), 0, 12),
    (("z0", "y", "z1"), 0, 13),
    (("y", "z0", "z1"), 0, 14),
)


def chain_kernel(
    bits, lengths, a_gain, a_bias, f_gain, f_bias, b_up, b_down,
    inputs, cotangent, w_in_hbm, w_out_hbm, w_up_hbm, w_down_hbm,
    outs_hbm, backs_hbm, gathered, vectors, keep_probs,
    w_in, w_out, w_up, w_down, states, backs, bias, ones, spread, stat, inv, xhat, normal, normal_t, qkv, turned,
    probs, recip, mixed_t, hidden, total, scratch, wide, d_mixed, d_scores, d_query_t,
    grads, landed, landed_vectors,
    load_sem, save_sem, stash_sem, swap_send, swap_recv, sum_send, sum_recv, sum_local, sum_free,
):
    section = lax.axis_index("section")
    group = lax.axis_index("dp")
    micro = section // 2
    side = section % 2
    axes = {"x": Axis("section", section, 1), "y": Axis("section", section, 2), "core": Axis("dp", group, 1)}
    for i in range(bits):
        axes["z%d" % i] = Axis("dp", group, 2 << i)
    used = []

    def load(src, dst):
        copy = pltpu.make_async_copy(src, dst, load_sem.at[len(used)])
        copy.start()
        used.append(copy)
        return copy

    def load_attention(layer):
        return [load(w_in_hbm.at[layer], w_in), load(w_out_hbm.at[layer], w_out)]

    def load_feed(layer):
        return [load(w_up_hbm.at[layer], w_up), load(w_down_hbm.at[layer], w_down)]

    def wait(copies):
        for copy in copies:
            copy.wait()

    def stash(index, src, dst):
        copy = pltpu.make_async_copy(src, dst, stash_sem.at[index])
        copy.start()
        return copy

    first = [load(inputs.at[micro], states.at[0])]
    attention_loads = load_attention(0)

    barrier = pltpu.get_barrier_semaphore()
    for axis in axes.values():
        pl.semaphore_signal(barrier, inc=1, device_id=axis.device, device_id_type=MESH)
    build_mask(lengths, micro, bias)
    ones[...] = jnp.ones_like(ones)
    width = states.shape[2]
    row = lax.broadcasted_iota(jnp.int32, spread.shape, 0) * HEAD
    lane = lax.broadcasted_iota(jnp.int32, spread.shape, 1)
    spread[...] = jnp.where((lane >= row) & (lane < row + HEAD), 1.0, 0.0)
    vectors[...] = jnp.zeros_like(vectors)
    sums = Sums(grads, landed, gathered, vectors, landed_vectors, axes, side, (sum_send, sum_recv, sum_local, sum_free))
    partner = section + 2 - 4 * micro
    kept = []

    def swap(index, src, dst):
        return pltpu.make_async_remote_copy(
            src_ref=src.at[partner + 1 - index], dst_ref=dst.at[0, micro],
            send_sem=swap_send.at[index], recv_sem=swap_recv.at[index],
            device_id=axes["y"].device, device_id_type=MESH,
        )

    outward, inward = swap(0, states, outs_hbm), swap(1, backs, backs_hbm)

    def start_swap(copy, sublayer):
        @pl.when(partner == sublayer)
        def _():
            copy.start()

    def local(src, dst):
        copy = pltpu.make_async_copy(src, dst, save_sem.at[len(kept)])
        copy.start()
        kept.append(copy)

    def norm(sublayer):
        layer = sublayer // 2
        gain, shift = (a_gain, a_bias) if sublayer % 2 == 0 else (f_gain, f_bias)
        return (
            ones, gain[layer : layer + 1, :], shift[layer : layer + 1, :], stat, inv.at[sublayer], xhat.at[sublayer]
        )

    wait(first)
    saved = {}
    feed_loads, last = [], []

    def weights_here(layer):
        attention_loads[0].wait()
        if layer == 0:
            feed_loads.extend(load_feed(0))
            last.append(load(cotangent.at[micro], backs.at[4]))

    for layer in range(2):
        if layer == 1:
            saved["probs"].wait()
        attention_forward(
            functools.partial(weights_here, layer), attention_loads[1].wait,
            states.at[2 * layer], norm(2 * layer), w_in, w_out, bias, normal, qkv.at[layer], turned, probs,
            recip.at[layer], scratch, mixed_t.at[layer], states.at[2 * layer + 1],
        )
        if layer == 0:
            pl.semaphore_wait(barrier, len(axes))
        start_swap(outward, 2 * layer)
        if layer == 0:
            saved["probs"] = stash(0, probs, keep_probs)
            attention_loads = load_attention(1)
        wait(feed_loads)
        if layer == 1:
            break
        feed_forward(
            states.at[1], norm(1), w_up, b_up[:1, :], w_down, b_down[:1, :],
            normal, hidden, scratch, total, states.at[2],
        )
        start_swap(outward, 1)
        feed_loads = load_feed(1)
    swapped = 2 * states.shape[1] * width
    sums.now = 16.5
    sums.occupy("y", swapped // 2)
    sums.now = 20.5
    wait(last)
    seen = []

    def ready(layer):
        def start(at, size):
            for first in range(at, at + size, PIECE):
                task = len(seen)
                order, after, rank = ORDERS[task % len(ORDERS)]
                sums.begin(sums.block(layer, first, min(PIECE, at + size - first), order, after, task), rank)
                seen.append(first)

        return start

    def produced():
        start_swap(outward, 3)
        local(states.at[section + 1], outs_hbm.at[0, micro])

    for layer in (1, 0):
        if layer == 1:
            feed_both(
                states.at[3], backs.at[4], norm(3), w_up, b_up.at[1:2, :], w_down, b_down[1:2, :],
                normal, normal_t, hidden, wide, d_mixed, scratch, total, states.at[4], backs.at[3],
                grads.at[1], vectors.at[1], side, sums.tick, ready(1), produced,
            )
        else:
            wait(feed_loads)
            feed_both(
                states.at[1], backs.at[2], norm(1), w_up, b_up.at[:1, :], w_down, b_down[:1, :],
                normal, normal_t, hidden, wide, d_mixed, scratch, total, None, backs.at[1],
                grads.at[0], vectors.at[0], side, sums.tick, ready(0), None,
            )
        start_swap(inward, 2 * layer + 1)
        sums.occupy("y", swapped // 2 * layer)
        if layer == 1:
            feed_loads = load_feed(0)
        else:
            wait(attention_loads)
            saved["probs"].wait()
        attention_backward(
            backs.at[2 * layer + 1], norm(2 * layer), w_in, w_out, normal, normal_t, qkv.at[layer], turned, probs,
            recip.at[layer], scratch, mixed_t.at[layer], spread, d_mixed, d_scores, d_query_t,
            wide.at[:, : qkv.shape[2]], total, backs.at[2 * layer], grads.at[layer], vectors.at[layer],
            side, sums.tick, ready(layer),
        )
        start_swap(inward, 2 * layer)
        sums.occupy("y", swapped // 2)
        sums.begin(sums.vector(layer), 0)
        if layer == 1:
            saved["probs"] = stash(1, keep_probs, probs)
            attention_loads = load_attention(0)
    local(backs.at[section], backs_hbm.at[0, micro])
    sums.drain()
    for copy in kept:
        copy.wait()
    outward.wait()
    inward.wait()


def run_chain(
    groups, inputs, cotangent, lengths, a_gain, a_bias, w_in, w_out, f_gain, f_bias, w_up, b_up, w_down, b_down
):
    _, count, width = inputs.shape
    layers, _, units = w_up.shape
    heads = width // HEAD
    bits = (groups // 2).bit_length() - 1
    vmem = pl.BlockSpec(memory_space=pltpu.VMEM)
    smem = pl.BlockSpec(memory_space=pltpu.SMEM)
    anywhere = pl.BlockSpec(memory_space=pl.ANY)
    shape = jax.ShapeDtypeStruct
    per_layer = 2 * width + units
    blocks = layers * (units // PIECE + 3)
    pushes = blocks * (3 * bits + 7) + layers * (bits + 2)
    return pl.pallas_call(
        functools.partial(chain_kernel, bits),
        out_shape=(
            shape((1, 2, count, width), BF16),
            shape((1, 2, count, width), BF16),
            shape((2, layers, width, per_layer), BF16),
            shape((layers, 16, width), F32),
            shape((heads, count, count), BF16),
        ),
        in_specs=[smem] + [vmem] * 6 + [anywhere] * 6,
        out_specs=[anywhere] * 3 + [vmem] + [anywhere],
        scratch_shapes=[
            pltpu.VMEM(w_in.shape[1:], BF16),
            pltpu.VMEM(w_out.shape[1:], BF16),
            pltpu.VMEM(w_up.shape[1:], BF16),
            pltpu.VMEM(w_down.shape[1:], BF16),
            pltpu.VMEM((2 * layers + 1, count, width), BF16),
            pltpu.VMEM((2 * layers + 1, count, width), BF16),
            pltpu.VMEM((count, count), F32),
            pltpu.VMEM((width, LANES), BF16),
            pltpu.VMEM((heads, width), F32),
            pltpu.VMEM((2, count, LANES), F32),
            pltpu.VMEM((2 * layers, count, LANES), F32),
            pltpu.VMEM((2 * layers, count, width), BF16),
            pltpu.VMEM((count, width), BF16),
            pltpu.VMEM((width, count), BF16),
            pltpu.VMEM((layers, count, 3 * width), BF16),
            pltpu.VMEM((width, count), BF16),
            pltpu.VMEM((heads, count, count), BF16),
            pltpu.VMEM((layers, heads, 8, count), F32),
            pltpu.VMEM((layers, width, count), BF16),
            pltpu.VMEM((count, units), BF16),
            pltpu.VMEM((count, width), F32),
            pltpu.VMEM((2, count, CHUNK), F32),
            pltpu.VMEM((count, 3 * width), BF16),
            pltpu.VMEM((count, width), BF16),
            pltpu.VMEM((2, count, count), BF16),
            pltpu.VMEM((PAIR, count), F32),
            pltpu.VMEM((layers, width, per_layer), BF16),
            pltpu.VMEM((layers, width, per_layer), BF16),
            pltpu.VMEM((layers, bits + 2, 16, width), F32),
            pltpu.SemaphoreType.DMA((14,)),
            pltpu.SemaphoreType.DMA((2,)),
            pltpu.SemaphoreType.DMA((2,)),
            pltpu.SemaphoreType.DMA((2,)),
            pltpu.SemaphoreType.DMA((2,)),
            pltpu.SemaphoreType.DMA((pushes,)),
            pltpu.SemaphoreType.DMA((pushes,)),
            pltpu.SemaphoreType.DMA((2 * blocks,)),
            pltpu.SemaphoreType.REGULAR((3 * blocks,)),
        ],
        compiler_params=pltpu.CompilerParams(
            vmem_limit_bytes=63 * 1024 * 1024, collective_id=0, has_side_effects=True
        ),
        cost_estimate=pl.CostEstimate(
            flops=30_000_000_000, bytes_accessed=50_000_000, transcendentals=10_000_000
        ),
        name="chain",
    )(lengths[:, 0, :], a_gain, a_bias, f_gain, f_bias, b_up, b_down, inputs, cotangent, w_in, w_out, w_up, w_down)


def widen_kernel(
    block, vectors, outs_in, backs_in,
    g_in, g_out, g_up, g_down, a_gain, a_bias, f_gain, f_bias, b_up, b_down, outs, backs,
):
    width = g_out.shape[2]
    quarter = width // 2
    third = 3 * quarter
    units = g_up.shape[2] // 2
    parts = units // width
    first = (pl.program_id(0) == 0) & (pl.program_id(1) == 0)
    outs[...] = outs_in[...]
    backs[...] = backs_in[...]

    @pl.when(first)
    def _():
        for i, ref in enumerate([a_gain, a_bias, f_gain, f_bias, b_down]):
            ref[...] = vectors[:, i, :]
        for i in range(b_up.shape[1] // width):
            b_up[:, i * width : (i + 1) * width] = vectors[:, 5 + i, :]

    for side in range(2):
        for part in range(3):
            at = part * width + side * quarter
            g_in[0, :, at : at + quarter] = block[side, 0, :, part * quarter : (part + 1) * quarter].astype(F32)
        at = third
        g_out[0, :, side * quarter : (side + 1) * quarter] = block[side, 0, :, at : at + quarter].astype(F32)
        at += quarter
        g_up[0, :, side * units : (side + 1) * units] = block[side, 0, :, at : at + units].astype(F32)
        at += units
        for i in range(parts):
            g_down[0, side * parts + i] = block[side, 0, :, at + i * width : at + (i + 1) * width].astype(F32)


def widen(gathered, vectors, outs, backs):
    _, layers, width, cols = gathered.shape
    units = (cols - 2 * width) // 2
    parts = 2 * units // width
    shape = jax.ShapeDtypeStruct
    steps = width // WIDEN_ROWS
    stream = pl.BlockSpec((1, 1, outs.shape[2] // steps, width), lambda i, j: (0, i, j, 0))
    small = pl.BlockSpec((layers, width), lambda i, j: (0, 0))
    g_in, g_out, g_up, g_down, *rest = pl.pallas_call(
        widen_kernel,
        grid=(layers, steps),
        out_shape=(
            shape((layers, width, 3 * width), F32),
            shape((layers, width, width), F32),
            shape((layers, width, 2 * units), F32),
            shape((layers, parts, width, width), F32),
        )
        + (shape((layers, width), F32),) * 4
        + (shape((layers, 2 * units), F32), shape((layers, width), F32))
        + (shape(outs.shape, BF16), shape(backs.shape, BF16)),
        in_specs=[
            pl.BlockSpec((2, 1, WIDEN_ROWS, cols), lambda i, j: (0, i, j, 0)),
            pl.BlockSpec(vectors.shape, lambda i, j: (0, 0, 0)),
            stream,
            stream,
        ],
        out_specs=(
            pl.BlockSpec((1, WIDEN_ROWS, 3 * width), lambda i, j: (i, j, 0)),
            pl.BlockSpec((1, WIDEN_ROWS, width), lambda i, j: (i, j, 0)),
            pl.BlockSpec((1, WIDEN_ROWS, 2 * units), lambda i, j: (i, j, 0)),
            pl.BlockSpec((1, parts, WIDEN_ROWS, width), lambda i, j: (i, 0, j, 0)),
        )
        + (small,) * 4
        + (pl.BlockSpec((layers, 2 * units), lambda i, j: (0, 0)), small, stream, stream),
        compiler_params=pltpu.CompilerParams(vmem_limit_bytes=60 * 1024 * 1024),
        name="widen",
    )(gathered, vectors, outs, backs)
    return (g_in, g_out, g_up, g_down.reshape(layers, 2 * units, width), *rest)


def body(
    groups, inputs, cotangent, clip_lengths, attention_gain, attention_bias, attention_in, attention_out,
    feed_gain, feed_bias, feed_up, feed_up_bias, feed_down, feed_down_bias,
):
    outs, backs, gathered, vectors = run_chain(
        groups, inputs, cotangent, clip_lengths, attention_gain, attention_bias, attention_in, attention_out,
        feed_gain, feed_bias, feed_up, feed_up_bias, feed_down, feed_down_bias,
    )[:4]
    g_in, g_out, g_up, g_down, a_gain, a_bias, f_gain, f_bias, b_up, b_down, outs, backs = widen(
        gathered, vectors, outs, backs
    )
    return outs, backs, a_gain, a_bias, g_in, g_out, f_gain, f_bias, g_up, b_up, g_down, b_down


def solution(mesh):
    return jax.shard_map(
        functools.partial(body, mesh.shape["dp"]),
        mesh=mesh,
        in_specs=(P(None, "dp", None), P(None, "dp", None), P(None, "dp", None)) + (P(),) * 10,
        out_specs=(P("section", None, "dp", None), P("section", None, "dp", None)) + (P(),) * 10,
        check_vma=False,
    )
```

```python
import functools

import jax
import jax.numpy as jnp
from jax import lax
from jax.experimental import pallas as pl
from jax.experimental.pallas import tpu as pltpu
from jax.sharding import PartitionSpec as P

HEAD = 64
PAIR = 2 * HEAD
LANES = 128
EPS = 1e-05
TANH_SCALE = 0.7978845608028654
CUBIC = 0.044715
MASKED = -1e30
QBLOCK = 256
ROWS = 128
WIDEN_ROWS = 128
CHUNK = 512
PIECE = 512
F32 = jnp.float32
BF16 = jnp.bfloat16
MESH = pl.DeviceIdType.MESH


def dot(left, right):
    return jnp.dot(left, right, preferred_element_type=F32)


def dot_nt(left, right):
    return lax.dot_general(left, right, (((1,), (1,)), ((), ())), preferred_element_type=F32)


def each(count, size, body, init=0):
    def step(i, carry):
        return body(pl.ds(pl.multiple_of(i * size, size), size), carry)

    return lax.fori_loop(0, count // size, step, init, unroll=True)


def fold(x, op):
    return op(x.reshape(x.shape[0] // 8, 8, x.shape[1]), axis=0)


def spans(count):
    return [(a, min(a + QBLOCK, count)) for a in range(0, count, QBLOCK)]


def tiles(width):
    return [slice(a, a + LANES) for a in range(0, width, LANES)]


def lane_half(shape, half):
    lane = lax.broadcasted_iota(jnp.int32, shape, 1)
    return (lane < HEAD) if half == 0 else (lane >= HEAD)


def norm_forward(src, ones, gain, shift, stat, inv, xhat, normal):
    count, width = src.shape
    stat[0] = dot(src[...], ones[...]) * (1.0 / width)

    def first(rows, carry):
        mean = stat[0, rows, :]
        for cols in tiles(width):
            centred = src[rows, cols].astype(F32) - mean
            normal[rows, cols] = (centred * centred).astype(BF16)
        return carry

    each(count, 64, first)
    inv[...] = lax.rsqrt(dot(normal[...], ones[...]) * (1.0 / width) + EPS)

    def second(rows, carry):
        mean, scale = stat[0, rows, :], inv[rows, :]
        for cols in tiles(width):
            value = (src[rows, cols].astype(F32) - mean) * scale
            xhat[rows, cols] = value.astype(BF16)
            normal[rows, cols] = (value * gain[:, cols] + shift[:, cols]).astype(BF16)
        return carry

    each(count, 64, second)


def norm_again(xhat, gain, shift, normal):
    def body(rows, carry):
        normal[rows, :] = (xhat[rows, :].astype(F32) * gain + shift).astype(BF16)
        return carry

    each(xhat.shape[0], 32, body)


def norm_backward(xhat, inv, ones, gain, d_normal, up, low, low_product, stat, dst):
    count, width = xhat.shape

    def first(rows, carry):
        sums = list(carry)
        for i, cols in enumerate(tiles(width)):
            grad = d_normal[rows, cols]
            value = xhat[rows, cols].astype(F32)
            product = grad * value
            low[rows, cols] = (grad * gain[:, cols]).astype(BF16)
            low_product[rows, cols] = (product * gain[:, cols]).astype(BF16)
            sums[2 * i] += fold(product, jnp.sum)
            sums[2 * i + 1] += fold(grad, jnp.sum)
        return tuple(sums)

    sums = each(count, 64, first, (jnp.zeros((8, LANES), F32),) * (2 * width // LANES))
    stat[0] = dot(low[...], ones[...]) * (1.0 / width)
    stat[1] = dot(low_product[...], ones[...]) * (1.0 / width)

    def second(rows, carry):
        mean, inner, scale = stat[0, rows, :], stat[1, rows, :], inv[rows, :]
        for cols in tiles(width):
            value = xhat[rows, cols].astype(F32)
            back = scale * (d_normal[rows, cols] * gain[:, cols] - mean - value * inner)
            dst[rows, cols] = (up[rows, cols].astype(F32) + back).astype(BF16)
        return carry

    each(count, 64, second)
    total = [jnp.sum(part, axis=0, keepdims=True) for part in sums]
    return jnp.concatenate(total[0::2], axis=1), jnp.concatenate(total[1::2], axis=1)


def gelu_pair(pre):
    square = pre * pre
    tanh_value = jnp.tanh(pre * (TANH_SCALE + (TANH_SCALE * CUBIC) * square))
    half = 0.5 + 0.5 * tanh_value
    value = pre * half
    slope = half + value * (1.0 - tanh_value) * (
        TANH_SCALE + (3.0 * CUBIC * TANH_SCALE) * square
    )
    return value, slope


def gelu(pre):
    return pre * (0.5 + 0.5 * jnp.tanh(pre * (TANH_SCALE + (TANH_SCALE * CUBIC) * pre * pre)))


def build_mask(lengths, micro, bias):
    count = bias.shape[0]
    ends = [lengths[micro, 0]]
    for i in range(1, lengths.shape[1] - 1):
        ends.append(ends[-1] + lengths[micro, i])
    query = lax.broadcasted_iota(jnp.int32, (1, count), 1)
    start = jnp.zeros((1, count), jnp.int32)
    for end in ends:
        start = jnp.where(query >= end, end, start)

    def step(i, carry):
        rows = pl.ds(pl.multiple_of(i * ROWS, ROWS), ROWS)
        key = lax.broadcasted_iota(jnp.int32, (ROWS, count), 0) + i * ROWS
        bias[rows, :] = jnp.where((key >= start) & (key <= query), 0.0, MASKED)
        return carry

    lax.fori_loop(0, count // ROWS, step, 0)


def attention_forward(in_here, out_here, src, norm, w_in, w_out, bias, normal, qkv, turned, probs, recip, scratch, mixed_t, dst):
    count, width = src.shape
    norm_forward(src, *norm, normal)
    in_here()
    for part in (1, 0, 2):
        cols = slice(part * width, (part + 1) * width)
        qkv[:, cols] = dot(normal[...], w_in[:, cols]).astype(BF16)
    turned[...] = jnp.transpose(qkv[:, 2 * width :])
    units = [(hp, half, a, b) for hp in range(width // PAIR) for a, b in spans(count) for half in range(2)]

    def scores(slot, unit):
        hp, half, a, b = unit
        lanes = slice(hp * PAIR, (hp + 1) * PAIR)
        query = qkv[a:b, lanes] * HEAD ** (-0.5)
        mine = jnp.where(lane_half(query.shape, half), query, 0).astype(BF16)
        scratch[slot, :b, : b - a] = dot_nt(qkv[:b, width + hp * PAIR : width + (hp + 1) * PAIR], mine)

    def finish(slot, unit):
        hp, half, a, b = unit
        span = b - a
        head = 2 * hp + half

        def first(rows, top):
            value = scratch[slot, rows, :span] + bias[rows, a:b]
            return jnp.maximum(top, fold(value, jnp.max))

        top = each(b, 64, first, jnp.full((8, span), MASKED, F32))
        top = jnp.max(top, axis=0, keepdims=True)

        def second(rows, summed):
            power = jnp.exp(scratch[slot, rows, :span] + bias[rows, a:b] - top)
            probs[head, rows, a:b] = power.astype(BF16)
            return summed + fold(power, jnp.sum)

        summed = each(b, 64, second, jnp.zeros((8, span), F32))
        scale = 1.0 / jnp.sum(summed, axis=0, keepdims=True)
        recip[head, :, a:b] = jnp.broadcast_to(scale, (8, span))
        rows = slice(head * HEAD, (head + 1) * HEAD)
        mixed_t[rows, a:b] = (dot(turned[rows, :b], probs[head, :b, a:b]) * scale).astype(BF16)

    for i, unit in enumerate(units):
        scores(i % 2, unit)
        if i:
            finish((i - 1) % 2, units[i - 1])
    finish((len(units) - 1) % 2, units[-1])
    out_here()
    branch = dot(jnp.transpose(mixed_t[...]), w_out[...])
    dst[...] = (src[...].astype(F32) + branch).astype(BF16)


def feed_forward(src, norm, w_up, b_up, w_down, b_down, normal, hidden, scratch, total, dst):
    count, width = src.shape
    chunks = hidden.shape[1] // CHUNK
    norm_forward(src, *norm, normal)

    def finish(i):
        def body(rows, carry):
            cols = slice(i * CHUNK, (i + 1) * CHUNK)
            hidden[rows, cols] = gelu(scratch[i % 2, rows, :] + b_up[:, cols]).astype(BF16)
            return carry

        each(count, 32, body)

    for i in range(chunks):
        scratch[i % 2] = dot(normal[...], w_up[:, i * CHUNK : (i + 1) * CHUNK])
        if i:
            finish(i - 1)
        if i == chunks - 1:
            total[...] = dot(hidden[:, : i * CHUNK], w_down[: i * CHUNK, :])
    finish(chunks - 1)
    done = (chunks - 1) * CHUNK
    branch = dot(hidden[:, done:], w_down[done:, :])
    dst[...] = (src[...].astype(F32) + b_down + total[...] + branch).astype(BF16)


def feed_both(
    src, up, norm, w_up, b_up, w_down, b_down, normal, normal_t, hidden, d_pre, other, scratch, total, dst, back,
    grads, vectors, side, tick, ready, produced,
):
    count, width = src.shape
    ones, gain, shift, stat, inv, xhat = norm
    units = hidden.shape[1]
    mine = units // 2
    base = 2 * width
    own = mine // CHUNK
    if produced is None:
        norm_again(xhat, gain, shift, normal)
    else:
        norm_forward(src, *norm, normal)
    normal_t[...] = jnp.transpose(normal[...])
    starts = [pl.multiple_of(side * mine, mine) + i * CHUNK for i in range(own)]
    starts += [pl.multiple_of((1 - side) * mine, mine) + i * CHUNK for i in range(own)]
    where = [pl.ds(pl.multiple_of(start, CHUNK), CHUNK) for start in starts]
    slots = d_pre.shape[1] // CHUNK
    place = [slice(i % slots * CHUNK, (i % slots + 1) * CHUNK) for i in range(2 * own)]

    def begin(i):
        scratch[0] = dot(normal[...], w_up[:, where[i]])
        scratch[1] = dot_nt(up[...], w_down[where[i], :])

    def finish(i):
        offset = b_up[:, where[i]]

        def body(rows, summed):
            value, grade = gelu_pair(scratch[0, rows, :] + offset)
            hidden[rows, where[i]] = value.astype(BF16)
            grad = (scratch[1, rows, :] * grade).astype(BF16)
            d_pre[rows, place[i]] = grad
            return summed + fold(grad.astype(F32), jnp.sum)

        summed = each(count, 32, body, jnp.zeros((8, CHUNK), F32))
        row = 5 + i % own + own * (side if i < own else 1 - side)
        vectors[pl.ds(row, 1), :] = jnp.sum(summed, axis=0, keepdims=True)

    def weights(i):
        grads[:, base + i * CHUNK : base + (i + 1) * CHUNK] = dot(normal_t[...], d_pre[:, place[i]]).astype(BF16)
        at = base + mine + i * width
        grads[:, at : at + width] = dot(jnp.transpose(hidden[:, where[i]]), up[...]).astype(BF16)

    def through(i):
        part = dot_nt(d_pre[:, place[i]], w_up[:, where[i]])
        total[...] = part if i == 0 else total[...] + part

    def send(i):
        ready(base + i * CHUNK, CHUNK)
        ready(base + mine + i * width, width)

    begin(0)
    finish(0)
    weights(0)
    tick(3.2)
    send(0)
    for i in range(1, 2 * own):
        begin(i)
        through(i - 1)
        finish(i)
        if i < own:
            weights(i)
            tick(2.2)
            send(i)
        else:
            tick(1.5)
    through(2 * own - 1)
    if produced is not None:
        branch = dot(hidden[...], w_down[...])
        dst[...] = (src[...].astype(F32) + b_down + branch).astype(BF16)
        produced()
    vectors[4:5, :] = jnp.sum(each(count, 64, lambda rows, s: s + fold(up[rows, :].astype(F32), jnp.sum),
                                   jnp.zeros((8, width), F32)), axis=0, keepdims=True)
    tick(1.5)
    d_gain, d_bias = norm_backward(xhat, inv, ones, gain, total, up, normal, other, stat, back)
    vectors[2:3, :] = d_gain
    vectors[3:4, :] = d_bias
    tick(1.0)


def attention_backward(
    up, norm, w_in, w_out, normal, normal_t, qkv, turned, probs, recip, scratch, mixed_t, spread,
    d_mixed, d_scores, d_query_t, d_qkv, total, dst, grads, vectors, side, tick, ready,
):
    count, width = up.shape
    ones, gain, shift, stat, inv, xhat = norm
    quarter = width // 2
    third = 3 * quarter
    cols = pl.ds(pl.multiple_of(side * quarter, quarter), quarter)
    grads[:, third : third + quarter] = dot(mixed_t[...], up[:, cols]).astype(BF16)
    tick(0.5)
    ready(third, quarter)
    norm_again(xhat, gain, shift, normal)
    normal_t[...] = jnp.transpose(normal[...])
    scratch[0] = dot_nt(up[...], w_out[...])
    scratch[1] = lax.dot_general(
        recip[:, 0, :], spread[...], (((0,), (0,)), ((), ())), precision=lax.Precision.HIGHEST, preferred_element_type=F32
    )

    def scaled(rows, carry):
        d_mixed[rows, :] = (scratch[0, rows, :] * scratch[1, rows, :]).astype(BF16)
        return carry

    each(count, 32, scaled)
    turned[...] = jnp.transpose(qkv[:, width : 2 * width])
    scale = HEAD ** (-0.5)

    def pair(hp):
        lanes = pl.multiple_of(hp * PAIR, PAIR)
        values = qkv[:, pl.ds(pl.multiple_of(2 * width + lanes, PAIR), PAIR)]
        units = [(half, a, b) for a, b in spans(count) for half in range(2)]

        def begin(slot, unit):
            half, a, b = unit
            part = d_mixed[a:b, pl.ds(lanes, PAIR)]
            mine = jnp.where(lane_half(part.shape, half), part, 0).astype(BF16)
            scratch[slot, :b, : b - a] = dot_nt(values[:b], mine)

        def finish(slot, unit):
            half, a, b = unit
            span = b - a
            head = 2 * hp + half

            def first(rows, summed):
                return summed + fold(scratch[slot, rows, :span] * probs[head, rows, a:b].astype(F32), jnp.sum)

            inner = each(b, 64, first, jnp.zeros((8, span), F32))
            inner = jnp.sum(inner, axis=0, keepdims=True) * recip[head, 0:1, a:b]

            def second(rows, carry):
                prob = probs[head, rows, a:b].astype(F32)
                d_scores[half, rows, a:b] = (prob * (scratch[slot, rows, :span] - inner)).astype(BF16)
                return carry

            each(b, 64, second)
            rows = pl.ds(pl.multiple_of(lanes + half * HEAD, HEAD), HEAD)
            d_query_t[half * HEAD : (half + 1) * HEAD, a:b] = dot(turned[rows, :b], d_scores[half, :b, a:b])

        for i, unit in enumerate(units):
            begin(i % 2, unit)
            if i:
                finish((i - 1) % 2, units[i - 1])
        finish((len(units) - 1) % 2, units[-1])
        d_qkv[:, pl.ds(lanes, PAIR)] = (jnp.transpose(d_query_t[...]) * scale).astype(BF16)
        query = qkv[:, pl.ds(lanes, PAIR)] * scale
        part = d_mixed[:, pl.ds(lanes, PAIR)]
        masks = [lane_half((count, PAIR), half) for half in range(2)]
        queries = [jnp.where(mask, query, 0).astype(BF16) for mask in masks]
        parts = [jnp.where(mask, part, 0).astype(BF16) for mask in masks]
        for a, b in spans(count):
            d_key = sum(dot(d_scores[half, a:b, a:], queries[half][a:]) for half in range(2))
            d_value = sum(dot(probs[2 * hp + half, a:b, a:], parts[half][a:]) for half in range(2))
            d_qkv[a:b, pl.ds(pl.multiple_of(width + lanes, PAIR), PAIR)] = d_key.astype(BF16)
            d_qkv[a:b, pl.ds(pl.multiple_of(2 * width + lanes, PAIR), PAIR)] = d_value.astype(BF16)

    pairs = width // PAIR
    for i in range(pairs):
        pair((side * (pairs // 2) + i) % pairs)
        tick(2.0)
        if i == pairs // 2 - 1:
            for part in range(3):
                cols = pl.ds(pl.multiple_of(part * width + side * quarter, quarter), quarter)
                grads[:, part * quarter : (part + 1) * quarter] = dot(normal_t[...], d_qkv[:, cols]).astype(BF16)
            tick(0.8)
            ready(0, third)
    total[...] = dot_nt(d_qkv[...], w_in[...])
    tick(0.9)
    d_gain, d_bias = norm_backward(xhat, inv, ones, gain, total, up, normal, d_mixed, stat, dst)
    vectors[0:1, :] = d_gain
    vectors[1:2, :] = d_bias
    tick(1.0)


class Axis:
    def __init__(self, name, index, step):
        self.bit = (index // step) % 2
        self.device = {name: index + step * (1 - 2 * self.bit)}


class Request:
    def __init__(self, src, dst, name):
        self.src, self.dst, self.name, self.copy = src, dst, name, None
        self.size = jnp.dtype(src.dtype).itemsize
        for extent in src.shape:
            self.size *= extent


class Sums:
    RATE, CORE_RATE, LAG, AHEAD, STEP, MARGIN = 85e3, 150e3, 1.0, 8.0, 0.3, 1.0

    def __init__(self, grads, landed, gathered, vectors, landed_vectors, axes, side, sems):
        self.grads, self.landed, self.gathered = grads, landed, gathered
        self.vectors, self.landed_vectors = vectors, landed_vectors
        self.axes, self.side = axes, side
        self.send_sem, self.recv_sem, self.local_sem, self.free_sem = sems
        self.depth = [name for name in axes if name[0] == "z"]
        self.used = self.count = 0
        self.sent, self.locals, self.active, self.queue = [], [], [], []
        self.free, self.now = {}, 0.0

    def loads(self, name, size):
        if name == "core":
            return {"core": size / self.CORE_RATE}
        if name[0] != "z":
            return {name: 2 * size / self.RATE}
        loads = {"z": 2 * size / self.RATE}
        if name != "z0":
            loads["mid"] = (2 << int(name[1:])) * size / self.RATE
        return loads

    def occupy(self, name, size):
        for key, load in self.loads(name, size).items():
            self.free[key] = max(self.now, self.free.get(key, 0.0)) + load

    def issue(self, request):
        request.copy = pltpu.make_async_remote_copy(
            src_ref=request.src, dst_ref=request.dst,
            send_sem=self.send_sem.at[self.used], recv_sem=self.recv_sem.at[self.used],
            device_id=self.axes[request.name].device, device_id_type=MESH,
        )
        request.copy.start()
        self.used += 1
        self.sent.append(request.copy)
        self.occupy(request.name, request.size)
        return max(self.free[key] for key in self.loads(request.name, request.size)) + self.LAG

    def open_at(self, request):
        return max(self.free.get(key, 0.0) for key in self.loads(request.name, request.size)) - self.AHEAD

    def dispatch(self):
        for entry in sorted(self.queue, key=lambda entry: entry[:2]):
            if self.open_at(entry[2]) <= self.now:
                self.queue.remove(entry)
                group = entry[3]
                group["over"] = max(group["over"], self.issue(entry[2]))
                group["left"] -= 1
                if not group["left"]:
                    self.active.append((group["over"], entry[0], self.count, group["task"]))
                    self.count += 1

    def step(self, task, rank):
        requests = next(task, None)
        if requests is not None:
            group = {"left": len(requests), "over": 0.0, "task": task}
            for request in requests:
                self.queue.append((rank, self.count, request, group))
                self.count += 1

    def begin(self, task, rank):
        self.step(task, rank)
        self.dispatch()

    def tick(self, spent):
        self.now += spent
        stolen = 0.0
        self.dispatch()
        while self.active:
            entry = min(self.active, key=lambda entry: entry[:3])
            if entry[0] + self.MARGIN > self.now:
                break
            self.active.remove(entry)
            self.step(entry[3], entry[1])
            self.dispatch()
            stolen += self.STEP
        self.now += stolen

    def drain(self):
        while self.active or self.queue:
            self.dispatch()
            opens = min([self.open_at(entry[2]) for entry in self.queue], default=float("inf"))
            entry = min(self.active, key=lambda entry: entry[:3], default=None)
            if entry is None or self.now < opens < entry[0]:
                self.now = opens
                continue
            self.now = max(self.now, entry[0]) + self.STEP
            self.active.remove(entry)
            self.step(entry[3], entry[1])
        for copy in self.sent:
            copy.wait_send()
        for copy in self.locals:
            copy.wait()

    def done(self, copy):
        copy.wait_send()
        self.sent = [other for other in self.sent if other is not copy]

    def block(self, layer, start, size, order, after, task):
        cols = slice(start, start + size)
        here = lambda at, rows: self.grads.at[layer, pl.ds(pl.multiple_of(at, 16), rows), cols]
        at, rows, land, path = 0, self.grads.shape[1], 0, []
        half = rows // 2
        base = self.axes["core"].bit * half
        spare = lambda at, rows: self.landed.at[layer, pl.ds(pl.multiple_of(at, 16), rows), cols]
        there = lambda side: self.gathered.at[side, layer, pl.ds(pl.multiple_of(base, 16), half), cols]
        names = ["core"]
        for name in order:
            names += self.depth[1:] if name == "z1" else [name]
        for i, name in enumerate(names):
            bit = self.axes[name].bit
            last = i == len(names) - 1
            halve = not last and rows % 32 == 0
            keep = rows // 2 if halve else rows
            mine = at + bit * keep if halve else at
            away = at + (1 - bit) * keep if halve else at
            push = Request(here(away, keep), spare(land, keep), name)
            yield [push]
            push.copy.wait_recv()
            if not halve:
                self.done(push.copy)
            elif i:
                path.append((name, mine, keep))
            total = (here(mine, keep)[...].astype(F32) + spare(land, keep)[...].astype(F32)).astype(BF16)
            if last:
                spare(mine - base, keep)[...] = total
            else:
                here(mine, keep)[...] = total
            land += keep
            at, rows = mine, keep
        path = path[::-1]
        turn = len(path) - after
        for k, name in enumerate(["x"] + [step[0] for step in path[turn:]]):
            pl.semaphore_signal(
                self.free_sem.at[3 * task + k], inc=1, device_id=self.axes[name].device, device_id_type=MESH
            )
        at = at - base
        for name, mine, keep in path[:turn]:
            at = mine - base
            push = Request(spare(at, keep), spare(at, keep), name)
            yield [push]
            push.copy.wait_recv()
        if turn:
            at, rows = (path[turn][1] - base, path[turn][2]) if after else (0, half)

        def save(index, side):
            src = spare(index * half, half)
            copy = pltpu.make_async_copy(src, there(side), self.local_sem.at[2 * task + index])
            copy.start()
            self.locals.append(copy)
            return Request(src, there(side), "core")

        if not after:
            near = save(0, self.side)
        pl.semaphore_wait(self.free_sem.at[3 * task], 1)
        push = Request(spare(at, rows), spare(half + at, rows), "x")
        yield [push]
        push.copy.wait_recv()
        for k, (name, mine, keep) in enumerate(path[turn:]):
            pl.semaphore_wait(self.free_sem.at[3 * task + k + 1], 1)
            pushes = [Request(spare(at, keep), spare(at, keep), name) for at in (mine - base, half + mine - base)]
            yield pushes
            for push in pushes:
                push.copy.wait_recv()
        if after:
            near = save(0, self.side)
        far = save(1, 1 - self.side)
        yield [near, far]
        near.copy.wait_recv()
        far.copy.wait_recv()

    def vector(self, layer):
        for i, name in enumerate(["core", "y"] + self.depth):
            push = Request(self.vectors.at[layer], self.landed_vectors.at[layer, i], name)
            yield [push]
            push.copy.wait_recv()
            self.done(push.copy)
            self.vectors[layer] = self.vectors[layer] + self.landed_vectors[layer, i]


ORDERS = (
    (("z0", "z1", "y"), 0, 1),
    (("y", "z0", "z1"), 0, 2),
    (("z0", "y", "z1"), 0, 3),
    (("z0", "z1", "y"), 0, 4),
    (("y", "z0", "z1"), 2, 5),
    (("z0", "z1", "y"), 0, 6),
    (("y", "z1", "z0"), 1, 7),
    (("z0", "y", "z1"), 2, 8),
    (("y", "z0", "z1"), 0, 9),
    (("z0", "z1", "y"), 1, 10),
    (("y", "z0", "z1"), 1, 11),
    (("z0", "y", "z1"), 1, 12),
    (("y", "z1", "z0"), 0, 13),
    (("y", "z0", "z1"), 2, 14),
)


def chain_kernel(
    bits, lengths, a_gain, a_bias, f_gain, f_bias, b_up, b_down,
    inputs, cotangent, w_in_hbm, w_out_hbm, w_up_hbm, w_down_hbm,
    outs_hbm, backs_hbm, gathered, vectors, keep_probs,
    w_in, w_out, w_up, w_down, states, backs, bias, ones, spread, stat, inv, xhat, normal, normal_t, qkv, turned,
    probs, recip, mixed_t, hidden, total, scratch, wide, d_mixed, d_scores, d_query_t,
    grads, landed, landed_vectors,
    load_sem, save_sem, stash_sem, swap_send, swap_recv, sum_send, sum_recv, sum_local, sum_free,
):
    section = lax.axis_index("section")
    group = lax.axis_index("dp")
    micro = section // 2
    side = section % 2
    axes = {"x": Axis("section", section, 1), "y": Axis("section", section, 2), "core": Axis("dp", group, 1)}
    for i in range(bits):
        axes["z%d" % i] = Axis("dp", group, 2 << i)
    used = []

    def load(src, dst):
        copy = pltpu.make_async_copy(src, dst, load_sem.at[len(used)])
        copy.start()
        used.append(copy)
        return copy

    def load_attention(layer):
        return [load(w_in_hbm.at[layer], w_in), load(w_out_hbm.at[layer], w_out)]

    def load_feed(layer):
        return [load(w_up_hbm.at[layer], w_up), load(w_down_hbm.at[layer], w_down)]

    def wait(copies):
        for copy in copies:
            copy.wait()

    def stash(index, src, dst):
        copy = pltpu.make_async_copy(src, dst, stash_sem.at[index])
        copy.start()
        return copy

    first = [load(inputs.at[micro], states.at[0])]
    attention_loads = load_attention(0)

    barrier = pltpu.get_barrier_semaphore()
    for axis in axes.values():
        pl.semaphore_signal(barrier, inc=1, device_id=axis.device, device_id_type=MESH)
    build_mask(lengths, micro, bias)
    ones[...] = jnp.ones_like(ones)
    width = states.shape[2]
    row = lax.broadcasted_iota(jnp.int32, spread.shape, 0) * HEAD
    lane = lax.broadcasted_iota(jnp.int32, spread.shape, 1)
    spread[...] = jnp.where((lane >= row) & (lane < row + HEAD), 1.0, 0.0)
    vectors[...] = jnp.zeros_like(vectors)
    sums = Sums(grads, landed, gathered, vectors, landed_vectors, axes, side, (sum_send, sum_recv, sum_local, sum_free))
    partner = section + 2 - 4 * micro
    kept = []

    def swap(index, src, dst):
        return pltpu.make_async_remote_copy(
            src_ref=src.at[partner + 1 - index], dst_ref=dst.at[0, micro],
            send_sem=swap_send.at[index], recv_sem=swap_recv.at[index],
            device_id=axes["y"].device, device_id_type=MESH,
        )

    outward, inward = swap(0, states, outs_hbm), swap(1, backs, backs_hbm)

    def start_swap(copy, sublayer):
        @pl.when(partner == sublayer)
        def _():
            copy.start()

    def local(src, dst):
        copy = pltpu.make_async_copy(src, dst, save_sem.at[len(kept)])
        copy.start()
        kept.append(copy)

    def norm(sublayer):
        layer = sublayer // 2
        gain, shift = (a_gain, a_bias) if sublayer % 2 == 0 else (f_gain, f_bias)
        return (
            ones, gain[layer : layer + 1, :], shift[layer : layer + 1, :], stat, inv.at[sublayer], xhat.at[sublayer]
        )

    wait(first)
    saved = {}
    feed_loads, last = [], []

    def weights_here(layer):
        attention_loads[0].wait()
        if layer == 0:
            feed_loads.extend(load_feed(0))
            last.append(load(cotangent.at[micro], backs.at[4]))

    for layer in range(2):
        if layer == 1:
            saved["probs"].wait()
        attention_forward(
            functools.partial(weights_here, layer), attention_loads[1].wait,
            states.at[2 * layer], norm(2 * layer), w_in, w_out, bias, normal, qkv.at[layer], turned, probs,
            recip.at[layer], scratch, mixed_t.at[layer], states.at[2 * layer + 1],
        )
        if layer == 0:
            pl.semaphore_wait(barrier, len(axes))
        start_swap(outward, 2 * layer)
        if layer == 0:
            saved["probs"] = stash(0, probs, keep_probs)
            attention_loads = load_attention(1)
        wait(feed_loads)
        if layer == 1:
            break
        feed_forward(
            states.at[1], norm(1), w_up, b_up[:1, :], w_down, b_down[:1, :],
            normal, hidden, scratch, total, states.at[2],
        )
        start_swap(outward, 1)
        feed_loads = load_feed(1)
    swapped = 2 * states.shape[1] * width
    sums.now = 16.5
    sums.occupy("y", swapped // 2)
    sums.now = 20.5
    wait(last)
    seen = []

    def ready(layer):
        def start(at, size):
            for first in range(at, at + size, PIECE):
                task = len(seen)
                order, after, rank = ORDERS[task % len(ORDERS)]
                sums.begin(sums.block(layer, first, min(PIECE, at + size - first), order, after, task), rank)
                seen.append(first)

        return start

    def produced():
        start_swap(outward, 3)
        local(states.at[section + 1], outs_hbm.at[0, micro])

    for layer in (1, 0):
        if layer == 1:
            feed_both(
                states.at[3], backs.at[4], norm(3), w_up, b_up.at[1:2, :], w_down, b_down[1:2, :],
                normal, normal_t, hidden, wide, d_mixed, scratch, total, states.at[4], backs.at[3],
                grads.at[1], vectors.at[1], side, sums.tick, ready(1), produced,
            )
        else:
            wait(feed_loads)
            feed_both(
                states.at[1], backs.at[2], norm(1), w_up, b_up.at[:1, :], w_down, b_down[:1, :],
                normal, normal_t, hidden, wide, d_mixed, scratch, total, None, backs.at[1],
                grads.at[0], vectors.at[0], side, sums.tick, ready(0), None,
            )
        start_swap(inward, 2 * layer + 1)
        sums.occupy("y", swapped // 2 * layer)
        if layer == 1:
            feed_loads = load_feed(0)
        else:
            wait(attention_loads)
            saved["probs"].wait()
        attention_backward(
            backs.at[2 * layer + 1], norm(2 * layer), w_in, w_out, normal, normal_t, qkv.at[layer], turned, probs,
            recip.at[layer], scratch, mixed_t.at[layer], spread, d_mixed, d_scores, d_query_t,
            wide.at[:, : qkv.shape[2]], total, backs.at[2 * layer], grads.at[layer], vectors.at[layer],
            side, sums.tick, ready(layer),
        )
        start_swap(inward, 2 * layer)
        sums.occupy("y", swapped // 2)
        sums.begin(sums.vector(layer), 0)
        if layer == 1:
            saved["probs"] = stash(1, keep_probs, probs)
            attention_loads = load_attention(0)
    local(backs.at[section], backs_hbm.at[0, micro])
    sums.drain()
    for copy in kept:
        copy.wait()
    outward.wait()
    inward.wait()


def run_chain(
    groups, inputs, cotangent, lengths, a_gain, a_bias, w_in, w_out, f_gain, f_bias, w_up, b_up, w_down, b_down
):
    _, count, width = inputs.shape
    layers, _, units = w_up.shape
    heads = width // HEAD
    bits = (groups // 2).bit_length() - 1
    vmem = pl.BlockSpec(memory_space=pltpu.VMEM)
    smem = pl.BlockSpec(memory_space=pltpu.SMEM)
    anywhere = pl.BlockSpec(memory_space=pl.ANY)
    shape = jax.ShapeDtypeStruct
    per_layer = 2 * width + units
    blocks = layers * (units // PIECE + 3)
    pushes = blocks * (3 * bits + 7) + layers * (bits + 2)
    return pl.pallas_call(
        functools.partial(chain_kernel, bits),
        out_shape=(
            shape((1, 2, count, width), BF16),
            shape((1, 2, count, width), BF16),
            shape((2, layers, width, per_layer), BF16),
            shape((layers, 16, width), F32),
            shape((heads, count, count), BF16),
        ),
        in_specs=[smem] + [vmem] * 6 + [anywhere] * 6,
        out_specs=[anywhere] * 3 + [vmem] + [anywhere],
        scratch_shapes=[
            pltpu.VMEM(w_in.shape[1:], BF16),
            pltpu.VMEM(w_out.shape[1:], BF16),
            pltpu.VMEM(w_up.shape[1:], BF16),
            pltpu.VMEM(w_down.shape[1:], BF16),
            pltpu.VMEM((2 * layers + 1, count, width), BF16),
            pltpu.VMEM((2 * layers + 1, count, width), BF16),
            pltpu.VMEM((count, count), F32),
            pltpu.VMEM((width, LANES), BF16),
            pltpu.VMEM((heads, width), F32),
            pltpu.VMEM((2, count, LANES), F32),
            pltpu.VMEM((2 * layers, count, LANES), F32),
            pltpu.VMEM((2 * layers, count, width), BF16),
            pltpu.VMEM((count, width), BF16),
            pltpu.VMEM((width, count), BF16),
            pltpu.VMEM((layers, count, 3 * width), BF16),
            pltpu.VMEM((width, count), BF16),
            pltpu.VMEM((heads, count, count), BF16),
            pltpu.VMEM((layers, heads, 8, count), F32),
            pltpu.VMEM((layers, width, count), BF16),
            pltpu.VMEM((count, units), BF16),
            pltpu.VMEM((count, width), F32),
            pltpu.VMEM((2, count, CHUNK), F32),
            pltpu.VMEM((count, 3 * width), BF16),
            pltpu.VMEM((count, width), BF16),
            pltpu.VMEM((2, count, count), BF16),
            pltpu.VMEM((PAIR, count), F32),
            pltpu.VMEM((layers, width, per_layer), BF16),
            pltpu.VMEM((layers, width, per_layer), BF16),
            pltpu.VMEM((layers, bits + 2, 16, width), F32),
            pltpu.SemaphoreType.DMA((14,)),
            pltpu.SemaphoreType.DMA((2,)),
            pltpu.SemaphoreType.DMA((2,)),
            pltpu.SemaphoreType.DMA((2,)),
            pltpu.SemaphoreType.DMA((2,)),
            pltpu.SemaphoreType.DMA((pushes,)),
            pltpu.SemaphoreType.DMA((pushes,)),
            pltpu.SemaphoreType.DMA((2 * blocks,)),
            pltpu.SemaphoreType.REGULAR((3 * blocks,)),
        ],
        compiler_params=pltpu.CompilerParams(
            vmem_limit_bytes=63 * 1024 * 1024, collective_id=0, has_side_effects=True
        ),
        cost_estimate=pl.CostEstimate(
            flops=30_000_000_000, bytes_accessed=50_000_000, transcendentals=10_000_000
        ),
        name="chain",
    )(lengths[:, 0, :], a_gain, a_bias, f_gain, f_bias, b_up, b_down, inputs, cotangent, w_in, w_out, w_up, w_down)


def widen_kernel(
    block, vectors, outs_in, backs_in,
    g_in, g_out, g_up, g_down, a_gain, a_bias, f_gain, f_bias, b_up, b_down, outs, backs,
):
    width = g_out.shape[2]
    quarter = width // 2
    third = 3 * quarter
    units = g_up.shape[2] // 2
    parts = units // width
    first = (pl.program_id(0) == 0) & (pl.program_id(1) == 0)
    outs[...] = outs_in[...]
    backs[...] = backs_in[...]

    @pl.when(first)
    def _():
        for i, ref in enumerate([a_gain, a_bias, f_gain, f_bias, b_down]):
            ref[...] = vectors[:, i, :]
        for i in range(b_up.shape[1] // width):
            b_up[:, i * width : (i + 1) * width] = vectors[:, 5 + i, :]

    for side in range(2):
        for part in range(3):
            at = part * width + side * quarter
            g_in[0, :, at : at + quarter] = block[side, 0, :, part * quarter : (part + 1) * quarter].astype(F32)
        at = third
        g_out[0, :, side * quarter : (side + 1) * quarter] = block[side, 0, :, at : at + quarter].astype(F32)
        at += quarter
        g_up[0, :, side * units : (side + 1) * units] = block[side, 0, :, at : at + units].astype(F32)
        at += units
        for i in range(parts):
            g_down[0, side * parts + i] = block[side, 0, :, at + i * width : at + (i + 1) * width].astype(F32)


def widen(gathered, vectors, outs, backs):
    _, layers, width, cols = gathered.shape
    units = (cols - 2 * width) // 2
    parts = 2 * units // width
    shape = jax.ShapeDtypeStruct
    steps = width // WIDEN_ROWS
    stream = pl.BlockSpec((1, 1, outs.shape[2] // steps, width), lambda i, j: (0, i, j, 0))
    small = pl.BlockSpec((layers, width), lambda i, j: (0, 0))
    g_in, g_out, g_up, g_down, *rest = pl.pallas_call(
        widen_kernel,
        grid=(layers, steps),
        out_shape=(
            shape((layers, width, 3 * width), F32),
            shape((layers, width, width), F32),
            shape((layers, width, 2 * units), F32),
            shape((layers, parts, width, width), F32),
        )
        + (shape((layers, width), F32),) * 4
        + (shape((layers, 2 * units), F32), shape((layers, width), F32))
        + (shape(outs.shape, BF16), shape(backs.shape, BF16)),
        in_specs=[
            pl.BlockSpec((2, 1, WIDEN_ROWS, cols), lambda i, j: (0, i, j, 0)),
            pl.BlockSpec(vectors.shape, lambda i, j: (0, 0, 0)),
            stream,
            stream,
        ],
        out_specs=(
            pl.BlockSpec((1, WIDEN_ROWS, 3 * width), lambda i, j: (i, j, 0)),
            pl.BlockSpec((1, WIDEN_ROWS, width), lambda i, j: (i, j, 0)),
            pl.BlockSpec((1, WIDEN_ROWS, 2 * units), lambda i, j: (i, j, 0)),
            pl.BlockSpec((1, parts, WIDEN_ROWS, width), lambda i, j: (i, 0, j, 0)),
        )
        + (small,) * 4
        + (pl.BlockSpec((layers, 2 * units), lambda i, j: (0, 0)), small, stream, stream),
        compiler_params=pltpu.CompilerParams(vmem_limit_bytes=60 * 1024 * 1024),
        name="widen",
    )(gathered, vectors, outs, backs)
    return (g_in, g_out, g_up, g_down.reshape(layers, 2 * units, width), *rest)


def body(
    groups, inputs, cotangent, clip_lengths, attention_gain, attention_bias, attention_in, attention_out,
    feed_gain, feed_bias, feed_up, feed_up_bias, feed_down, feed_down_bias,
):
    outs, backs, gathered, vectors = run_chain(
        groups, inputs, cotangent, clip_lengths, attention_gain, attention_bias, attention_in, attention_out,
        feed_gain, feed_bias, feed_up, feed_up_bias, feed_down, feed_down_bias,
    )[:4]
    g_in, g_out, g_up, g_down, a_gain, a_bias, f_gain, f_bias, b_up, b_down, outs, backs = widen(
        gathered, vectors, outs, backs
    )
    return outs, backs, a_gain, a_bias, g_in, g_out, f_gain, f_bias, g_up, b_up, g_down, b_down


def solution(mesh):
    return jax.shard_map(
        functools.partial(body, mesh.shape["dp"]),
        mesh=mesh,
        in_specs=(P(None, "dp", None), P(None, "dp", None), P(None, "dp", None)) + (P(),) * 10,
        out_specs=(P("section", None, "dp", None), P("section", None, "dp", None)) + (P(),) * 10,
        check_vma=False,
    )
```

```python
import functools

import jax
import jax.numpy as jnp
from jax import lax
from jax.experimental import pallas as pl
from jax.experimental.pallas import tpu as pltpu
from jax.sharding import PartitionSpec as P

HEAD = 64
PAIR = 2 * HEAD
LANES = 128
EPS = 1e-05
TANH_SCALE = 0.7978845608028654
CUBIC = 0.044715
MASKED = -1e30
QBLOCK = 256
ROWS = 128
WIDEN_ROWS = 128
CHUNK = 512
PIECE = 512
F32 = jnp.float32
BF16 = jnp.bfloat16
MESH = pl.DeviceIdType.MESH


def dot(left, right):
    return jnp.dot(left, right, preferred_element_type=F32)


def dot_nt(left, right):
    return lax.dot_general(left, right, (((1,), (1,)), ((), ())), preferred_element_type=F32)


def each(count, size, body, init=0):
    def step(i, carry):
        return body(pl.ds(pl.multiple_of(i * size, size), size), carry)

    return lax.fori_loop(0, count // size, step, init, unroll=True)


def fold(x, op):
    return op(x.reshape(x.shape[0] // 8, 8, x.shape[1]), axis=0)


def spans(count):
    return [(a, min(a + QBLOCK, count)) for a in range(0, count, QBLOCK)]


def tiles(width):
    return [slice(a, a + LANES) for a in range(0, width, LANES)]


def lane_half(shape, half):
    lane = lax.broadcasted_iota(jnp.int32, shape, 1)
    return (lane < HEAD) if half == 0 else (lane >= HEAD)


def norm_forward(src, ones, gain, shift, stat, inv, xhat, normal):
    count, width = src.shape
    stat[0] = dot(src[...], ones[...]) * (1.0 / width)

    def first(rows, carry):
        mean = stat[0, rows, :]
        for cols in tiles(width):
            centred = src[rows, cols].astype(F32) - mean
            normal[rows, cols] = (centred * centred).astype(BF16)
        return carry

    each(count, 64, first)
    inv[...] = lax.rsqrt(dot(normal[...], ones[...]) * (1.0 / width) + EPS)

    def second(rows, carry):
        mean, scale = stat[0, rows, :], inv[rows, :]
        for cols in tiles(width):
            value = (src[rows, cols].astype(F32) - mean) * scale
            xhat[rows, cols] = value.astype(BF16)
            normal[rows, cols] = (value * gain[:, cols] + shift[:, cols]).astype(BF16)
        return carry

    each(count, 64, second)


def norm_again(xhat, gain, shift, normal):
    def body(rows, carry):
        normal[rows, :] = (xhat[rows, :].astype(F32) * gain + shift).astype(BF16)
        return carry

    each(xhat.shape[0], 32, body)


def norm_backward(xhat, inv, ones, gain, d_normal, up, low, low_product, stat, dst):
    count, width = xhat.shape

    def first(rows, carry):
        sums = list(carry)
        for i, cols in enumerate(tiles(width)):
            grad = d_normal[rows, cols]
            value = xhat[rows, cols].astype(F32)
            product = grad * value
            low[rows, cols] = (grad * gain[:, cols]).astype(BF16)
            low_product[rows, cols] = (product * gain[:, cols]).astype(BF16)
            sums[2 * i] += fold(product, jnp.sum)
            sums[2 * i + 1] += fold(grad, jnp.sum)
        return tuple(sums)

    sums = each(count, 64, first, (jnp.zeros((8, LANES), F32),) * (2 * width // LANES))
    stat[0] = dot(low[...], ones[...]) * (1.0 / width)
    stat[1] = dot(low_product[...], ones[...]) * (1.0 / width)

    def second(rows, carry):
        mean, inner, scale = stat[0, rows, :], stat[1, rows, :], inv[rows, :]
        for cols in tiles(width):
            value = xhat[rows, cols].astype(F32)
            back = scale * (d_normal[rows, cols] * gain[:, cols] - mean - value * inner)
            dst[rows, cols] = (up[rows, cols].astype(F32) + back).astype(BF16)
        return carry

    each(count, 64, second)
    total = [jnp.sum(part, axis=0, keepdims=True) for part in sums]
    return jnp.concatenate(total[0::2], axis=1), jnp.concatenate(total[1::2], axis=1)


def gelu_pair(pre):
    square = pre * pre
    tanh_value = jnp.tanh(pre * (TANH_SCALE + (TANH_SCALE * CUBIC) * square))
    half = 0.5 + 0.5 * tanh_value
    value = pre * half
    slope = half + value * (1.0 - tanh_value) * (
        TANH_SCALE + (3.0 * CUBIC * TANH_SCALE) * square
    )
    return value, slope


def gelu(pre):
    return pre * (0.5 + 0.5 * jnp.tanh(pre * (TANH_SCALE + (TANH_SCALE * CUBIC) * pre * pre)))


def build_mask(lengths, micro, bias):
    count = bias.shape[0]
    ends = [lengths[micro, 0]]
    for i in range(1, lengths.shape[1] - 1):
        ends.append(ends[-1] + lengths[micro, i])
    query = lax.broadcasted_iota(jnp.int32, (1, count), 1)
    start = jnp.zeros((1, count), jnp.int32)
    for end in ends:
        start = jnp.where(query >= end, end, start)

    def step(i, carry):
        rows = pl.ds(pl.multiple_of(i * ROWS, ROWS), ROWS)
        key = lax.broadcasted_iota(jnp.int32, (ROWS, count), 0) + i * ROWS
        bias[rows, :] = jnp.where((key >= start) & (key <= query), 0.0, MASKED)
        return carry

    lax.fori_loop(0, count // ROWS, step, 0)


def attention_forward(in_here, out_here, src, norm, w_in, w_out, bias, normal, qkv, turned, probs, recip, scratch, mixed_t, dst):
    count, width = src.shape
    norm_forward(src, *norm, normal)
    in_here()
    for part in (1, 0, 2):
        cols = slice(part * width, (part + 1) * width)
        qkv[:, cols] = dot(normal[...], w_in[:, cols]).astype(BF16)
    turned[...] = jnp.transpose(qkv[:, 2 * width :])
    units = [(hp, half, a, b) for hp in range(width // PAIR) for a, b in spans(count) for half in range(2)]

    def scores(slot, unit):
        hp, half, a, b = unit
        lanes = slice(hp * PAIR, (hp + 1) * PAIR)
        query = qkv[a:b, lanes] * HEAD ** (-0.5)
        mine = jnp.where(lane_half(query.shape, half), query, 0).astype(BF16)
        scratch[slot, :b, : b - a] = dot_nt(qkv[:b, width + hp * PAIR : width + (hp + 1) * PAIR], mine)

    def finish(slot, unit):
        hp, half, a, b = unit
        span = b - a
        head = 2 * hp + half

        def first(rows, top):
            value = scratch[slot, rows, :span] + bias[rows, a:b]
            return jnp.maximum(top, fold(value, jnp.max))

        top = each(b, 64, first, jnp.full((8, span), MASKED, F32))
        top = jnp.max(top, axis=0, keepdims=True)

        def second(rows, summed):
            power = jnp.exp(scratch[slot, rows, :span] + bias[rows, a:b] - top)
            probs[head, rows, a:b] = power.astype(BF16)
            return summed + fold(power, jnp.sum)

        summed = each(b, 64, second, jnp.zeros((8, span), F32))
        scale = 1.0 / jnp.sum(summed, axis=0, keepdims=True)
        recip[head, :, a:b] = jnp.broadcast_to(scale, (8, span))
        rows = slice(head * HEAD, (head + 1) * HEAD)
        mixed_t[rows, a:b] = (dot(turned[rows, :b], probs[head, :b, a:b]) * scale).astype(BF16)

    for i, unit in enumerate(units):
        scores(i % 2, unit)
        if i:
            finish((i - 1) % 2, units[i - 1])
    finish((len(units) - 1) % 2, units[-1])
    out_here()
    branch = dot(jnp.transpose(mixed_t[...]), w_out[...])
    dst[...] = (src[...].astype(F32) + branch).astype(BF16)


def feed_forward(src, norm, w_up, b_up, w_down, b_down, normal, hidden, scratch, total, dst):
    count, width = src.shape
    chunks = hidden.shape[1] // CHUNK
    norm_forward(src, *norm, normal)

    def finish(i):
        def body(rows, carry):
            cols = slice(i * CHUNK, (i + 1) * CHUNK)
            hidden[rows, cols] = gelu(scratch[i % 2, rows, :] + b_up[:, cols]).astype(BF16)
            return carry

        each(count, 32, body)

    for i in range(chunks):
        scratch[i % 2] = dot(normal[...], w_up[:, i * CHUNK : (i + 1) * CHUNK])
        if i:
            finish(i - 1)
        if i == chunks - 1:
            total[...] = dot(hidden[:, : i * CHUNK], w_down[: i * CHUNK, :])
    finish(chunks - 1)
    done = (chunks - 1) * CHUNK
    branch = dot(hidden[:, done:], w_down[done:, :])
    dst[...] = (src[...].astype(F32) + b_down + total[...] + branch).astype(BF16)


def feed_both(
    src, up, norm, w_up, b_up, w_down, b_down, normal, normal_t, hidden, d_pre, other, scratch, total, dst, back,
    grads, vectors, side, tick, ready, produced,
):
    count, width = src.shape
    ones, gain, shift, stat, inv, xhat = norm
    units = hidden.shape[1]
    mine = units // 2
    base = 2 * width
    own = mine // CHUNK
    if produced is None:
        norm_again(xhat, gain, shift, normal)
    else:
        norm_forward(src, *norm, normal)
    normal_t[...] = jnp.transpose(normal[...])
    starts = [pl.multiple_of(side * mine, mine) + i * CHUNK for i in range(own)]
    starts += [pl.multiple_of((1 - side) * mine, mine) + i * CHUNK for i in range(own)]
    where = [pl.ds(pl.multiple_of(start, CHUNK), CHUNK) for start in starts]
    slots = d_pre.shape[1] // CHUNK
    place = [slice(i % slots * CHUNK, (i % slots + 1) * CHUNK) for i in range(2 * own)]

    def begin(i):
        scratch[0] = dot(normal[...], w_up[:, where[i]])
        scratch[1] = dot_nt(up[...], w_down[where[i], :])

    def finish(i):
        offset = b_up[:, where[i]]

        def body(rows, summed):
            value, grade = gelu_pair(scratch[0, rows, :] + offset)
            hidden[rows, where[i]] = value.astype(BF16)
            grad = (scratch[1, rows, :] * grade).astype(BF16)
            d_pre[rows, place[i]] = grad
            return summed + fold(grad.astype(F32), jnp.sum)

        summed = each(count, 32, body, jnp.zeros((8, CHUNK), F32))
        row = 5 + i % own + own * (side if i < own else 1 - side)
        vectors[pl.ds(row, 1), :] = jnp.sum(summed, axis=0, keepdims=True)

    def weights(i):
        grads[:, base + i * CHUNK : base + (i + 1) * CHUNK] = dot(normal_t[...], d_pre[:, place[i]]).astype(BF16)
        at = base + mine + i * width
        grads[:, at : at + width] = dot(jnp.transpose(hidden[:, where[i]]), up[...]).astype(BF16)

    def through(i):
        part = dot_nt(d_pre[:, place[i]], w_up[:, where[i]])
        total[...] = part if i == 0 else total[...] + part

    def send(i):
        ready(base + i * CHUNK, CHUNK)
        ready(base + mine + i * width, width)

    begin(0)
    finish(0)
    weights(0)
    tick(3.2)
    send(0)
    for i in range(1, 2 * own):
        begin(i)
        through(i - 1)
        finish(i)
        if i < own:
            weights(i)
            tick(2.2)
            send(i)
        else:
            tick(1.5)
    through(2 * own - 1)
    if produced is not None:
        branch = dot(hidden[...], w_down[...])
        dst[...] = (src[...].astype(F32) + b_down + branch).astype(BF16)
        produced()
    vectors[4:5, :] = jnp.sum(each(count, 64, lambda rows, s: s + fold(up[rows, :].astype(F32), jnp.sum),
                                   jnp.zeros((8, width), F32)), axis=0, keepdims=True)
    tick(1.5)
    d_gain, d_bias = norm_backward(xhat, inv, ones, gain, total, up, normal, other, stat, back)
    vectors[2:3, :] = d_gain
    vectors[3:4, :] = d_bias
    tick(1.0)


def attention_backward(
    up, norm, w_in, w_out, normal, normal_t, qkv, turned, probs, recip, scratch, mixed_t, spread,
    d_mixed, d_scores, d_query_t, d_qkv, total, dst, grads, vectors, side, tick, ready,
):
    count, width = up.shape
    ones, gain, shift, stat, inv, xhat = norm
    quarter = width // 2
    third = 3 * quarter
    cols = pl.ds(pl.multiple_of(side * quarter, quarter), quarter)
    grads[:, third : third + quarter] = dot(mixed_t[...], up[:, cols]).astype(BF16)
    tick(0.5)
    ready(third, quarter)
    norm_again(xhat, gain, shift, normal)
    normal_t[...] = jnp.transpose(normal[...])
    scratch[0] = dot_nt(up[...], w_out[...])
    scratch[1] = lax.dot_general(
        recip[:, 0, :], spread[...], (((0,), (0,)), ((), ())), precision=lax.Precision.HIGHEST, preferred_element_type=F32
    )

    def scaled(rows, carry):
        d_mixed[rows, :] = (scratch[0, rows, :] * scratch[1, rows, :]).astype(BF16)
        return carry

    each(count, 32, scaled)
    turned[...] = jnp.transpose(qkv[:, width : 2 * width])
    scale = HEAD ** (-0.5)

    def pair(hp):
        lanes = pl.multiple_of(hp * PAIR, PAIR)
        values = qkv[:, pl.ds(pl.multiple_of(2 * width + lanes, PAIR), PAIR)]
        units = [(half, a, b) for a, b in spans(count) for half in range(2)]

        def begin(slot, unit):
            half, a, b = unit
            part = d_mixed[a:b, pl.ds(lanes, PAIR)]
            mine = jnp.where(lane_half(part.shape, half), part, 0).astype(BF16)
            scratch[slot, :b, : b - a] = dot_nt(values[:b], mine)

        def finish(slot, unit):
            half, a, b = unit
            span = b - a
            head = 2 * hp + half

            def first(rows, summed):
                return summed + fold(scratch[slot, rows, :span] * probs[head, rows, a:b].astype(F32), jnp.sum)

            inner = each(b, 64, first, jnp.zeros((8, span), F32))
            inner = jnp.sum(inner, axis=0, keepdims=True) * recip[head, 0:1, a:b]

            def second(rows, carry):
                prob = probs[head, rows, a:b].astype(F32)
                d_scores[half, rows, a:b] = (prob * (scratch[slot, rows, :span] - inner)).astype(BF16)
                return carry

            each(b, 64, second)
            rows = pl.ds(pl.multiple_of(lanes + half * HEAD, HEAD), HEAD)
            d_query_t[half * HEAD : (half + 1) * HEAD, a:b] = dot(turned[rows, :b], d_scores[half, :b, a:b])

        for i, unit in enumerate(units):
            begin(i % 2, unit)
            if i:
                finish((i - 1) % 2, units[i - 1])
        finish((len(units) - 1) % 2, units[-1])
        d_qkv[:, pl.ds(lanes, PAIR)] = (jnp.transpose(d_query_t[...]) * scale).astype(BF16)
        query = qkv[:, pl.ds(lanes, PAIR)] * scale
        part = d_mixed[:, pl.ds(lanes, PAIR)]
        masks = [lane_half((count, PAIR), half) for half in range(2)]
        queries = [jnp.where(mask, query, 0).astype(BF16) for mask in masks]
        parts = [jnp.where(mask, part, 0).astype(BF16) for mask in masks]
        for a, b in spans(count):
            d_key = sum(dot(d_scores[half, a:b, a:], queries[half][a:]) for half in range(2))
            d_value = sum(dot(probs[2 * hp + half, a:b, a:], parts[half][a:]) for half in range(2))
            d_qkv[a:b, pl.ds(pl.multiple_of(width + lanes, PAIR), PAIR)] = d_key.astype(BF16)
            d_qkv[a:b, pl.ds(pl.multiple_of(2 * width + lanes, PAIR), PAIR)] = d_value.astype(BF16)

    pairs = width // PAIR
    for i in range(pairs):
        pair((side * (pairs // 2) + i) % pairs)
        tick(2.0)
        if i == pairs // 2 - 1:
            for part in range(3):
                cols = pl.ds(pl.multiple_of(part * width + side * quarter, quarter), quarter)
                grads[:, part * quarter : (part + 1) * quarter] = dot(normal_t[...], d_qkv[:, cols]).astype(BF16)
            tick(0.8)
            ready(0, third)
    total[...] = dot_nt(d_qkv[...], w_in[...])
    tick(0.9)
    d_gain, d_bias = norm_backward(xhat, inv, ones, gain, total, up, normal, d_mixed, stat, dst)
    vectors[0:1, :] = d_gain
    vectors[1:2, :] = d_bias
    tick(1.0)


class Axis:
    def __init__(self, name, index, step):
        self.bit = (index // step) % 2
        self.device = {name: index + step * (1 - 2 * self.bit)}


class Request:
    def __init__(self, src, dst, name):
        self.src, self.dst, self.name, self.copy = src, dst, name, None
        self.size = jnp.dtype(src.dtype).itemsize
        for extent in src.shape:
            self.size *= extent


class Sums:
    RATE, CORE_RATE, LAG, AHEAD, STEP, MARGIN = 85e3, 100e3, 1.0, 4.0, 0.3, 1.0

    def __init__(self, grads, landed, gathered, vectors, landed_vectors, axes, side, sems):
        self.grads, self.landed, self.gathered = grads, landed, gathered
        self.vectors, self.landed_vectors = vectors, landed_vectors
        self.axes, self.side = axes, side
        self.send_sem, self.recv_sem, self.local_sem, self.free_sem = sems
        self.depth = [name for name in axes if name[0] == "z"]
        self.used = self.count = 0
        self.sent, self.locals, self.active, self.queue = [], [], [], []
        self.free, self.now = {}, 0.0

    def loads(self, name, size):
        if name == "core":
            return {"core": size / self.CORE_RATE}
        if name[0] != "z":
            return {name: 2 * size / self.RATE}
        loads = {"z": 2 * size / self.RATE}
        if name != "z0":
            loads["mid"] = (2 << int(name[1:])) * size / self.RATE
        return loads

    def occupy(self, name, size):
        for key, load in self.loads(name, size).items():
            self.free[key] = max(self.now, self.free.get(key, 0.0)) + load

    def issue(self, request):
        request.copy = pltpu.make_async_remote_copy(
            src_ref=request.src, dst_ref=request.dst,
            send_sem=self.send_sem.at[self.used], recv_sem=self.recv_sem.at[self.used],
            device_id=self.axes[request.name].device, device_id_type=MESH,
        )
        request.copy.start()
        self.used += 1
        self.sent.append(request.copy)
        self.occupy(request.name, request.size)
        return max(self.free[key] for key in self.loads(request.name, request.size)) + self.LAG

    def open_at(self, request):
        return max(self.free.get(key, 0.0) for key in self.loads(request.name, request.size)) - self.AHEAD

    def dispatch(self):
        for entry in sorted(self.queue, key=lambda entry: entry[:2]):
            if self.open_at(entry[2]) <= self.now:
                self.queue.remove(entry)
                group = entry[3]
                group["over"] = max(group["over"], self.issue(entry[2]))
                group["left"] -= 1
                if not group["left"]:
                    self.active.append((group["over"], entry[0], self.count, group["task"]))
                    self.count += 1

    def step(self, task, rank):
        requests = next(task, None)
        if requests is not None:
            group = {"left": len(requests), "over": 0.0, "task": task}
            for request in requests:
                self.queue.append((rank, self.count, request, group))
                self.count += 1

    def begin(self, task, rank):
        self.step(task, rank)
        self.dispatch()

    def tick(self, spent):
        self.now += spent
        stolen = 0.0
        self.dispatch()
        while self.active:
            entry = min(self.active, key=lambda entry: entry[:3])
            if entry[0] + self.MARGIN > self.now:
                break
            self.active.remove(entry)
            self.step(entry[3], entry[1])
            self.dispatch()
            stolen += self.STEP
        self.now += stolen

    def drain(self):
        while self.active or self.queue:
            self.dispatch()
            opens = min([self.open_at(entry[2]) for entry in self.queue], default=float("inf"))
            entry = min(self.active, key=lambda entry: entry[:3], default=None)
            if entry is None or self.now < opens < entry[0]:
                self.now = opens
                continue
            self.now = max(self.now, entry[0]) + self.STEP
            self.active.remove(entry)
            self.step(entry[3], entry[1])
        for copy in self.sent:
            copy.wait_send()
        for copy in self.locals:
            copy.wait()

    def done(self, copy):
        copy.wait_send()
        self.sent = [other for other in self.sent if other is not copy]

    def block(self, layer, start, size, order, after, task):
        cols = slice(start, start + size)
        here = lambda at, rows: self.grads.at[layer, pl.ds(pl.multiple_of(at, 16), rows), cols]
        at, rows, land, path = 0, self.grads.shape[1], 0, []
        half = rows // 2
        base = self.axes["core"].bit * half
        spare = lambda at, rows: self.landed.at[layer, pl.ds(pl.multiple_of(at, 16), rows), cols]
        there = lambda side: self.gathered.at[side, layer, pl.ds(pl.multiple_of(base, 16), half), cols]
        names = ["core"]
        for name in order:
            names += self.depth[1:] if name == "z1" else [name]
        for i, name in enumerate(names):
            bit = self.axes[name].bit
            last = i == len(names) - 1
            halve = not last and rows % 32 == 0
            keep = rows // 2 if halve else rows
            mine = at + bit * keep if halve else at
            away = at + (1 - bit) * keep if halve else at
            push = Request(here(away, keep), spare(land, keep), name)
            yield [push]
            push.copy.wait_recv()
            if not halve:
                self.done(push.copy)
            elif i:
                path.append((name, mine, keep))
            total = (here(mine, keep)[...].astype(F32) + spare(land, keep)[...].astype(F32)).astype(BF16)
            if last:
                spare(mine - base, keep)[...] = total
            else:
                here(mine, keep)[...] = total
            land += keep
            at, rows = mine, keep
        path = path[::-1]
        turn = len(path) - after
        for k, name in enumerate(["x"] + [step[0] for step in path[turn:]]):
            pl.semaphore_signal(
                self.free_sem.at[3 * task + k], inc=1, device_id=self.axes[name].device, device_id_type=MESH
            )
        at = at - base
        for name, mine, keep in path[:turn]:
            at = mine - base
            push = Request(spare(at, keep), spare(at, keep), name)
            yield [push]
            push.copy.wait_recv()
        if turn:
            at, rows = (path[turn][1] - base, path[turn][2]) if after else (0, half)

        def save(index, side):
            src = spare(index * half, half)
            copy = pltpu.make_async_copy(src, there(side), self.local_sem.at[2 * task + index])
            copy.start()
            self.locals.append(copy)
            return Request(src, there(side), "core")

        if not after:
            near = save(0, self.side)
        pl.semaphore_wait(self.free_sem.at[3 * task], 1)
        push = Request(spare(at, rows), spare(half + at, rows), "x")
        yield [push]
        push.copy.wait_recv()
        for k, (name, mine, keep) in enumerate(path[turn:]):
            pl.semaphore_wait(self.free_sem.at[3 * task + k + 1], 1)
            pushes = [Request(spare(at, keep), spare(at, keep), name) for at in (mine - base, half + mine - base)]
            yield pushes
            for push in pushes:
                push.copy.wait_recv()
        if after:
            near = save(0, self.side)
        far = save(1, 1 - self.side)
        yield [near, far]
        near.copy.wait_recv()
        far.copy.wait_recv()

    def vector(self, layer):
        for i, name in enumerate(["core", "y"] + self.depth):
            push = Request(self.vectors.at[layer], self.landed_vectors.at[layer, i], name)
            yield [push]
            push.copy.wait_recv()
            self.done(push.copy)
            self.vectors[layer] = self.vectors[layer] + self.landed_vectors[layer, i]


ORDERS = (
    (("y", "z0", "z1"), 0, 1),
    (("y", "z1", "z0"), 1, 2),
    (("y", "z0", "z1"), 0, 3),
    (("y", "z0", "z1"), 0, 4),
    (("z0", "z1", "y"), 0, 5),
    (("z0", "z1", "y"), 0, 6),
    (("z0", "z1", "y"), 1, 7),
    (("z0", "y", "z1"), 2, 8),
    (("y", "z0", "z1"), 0, 9),
    (("y", "z0", "z1"), 1, 10),
    (("z0", "y", "z1"), 2, 11),
    (("z0", "z1", "y"), 0, 12),
    (("y", "z0", "z1"), 1, 13),
    (("z0", "z1", "y"), 0, 14),
)


def chain_kernel(
    bits, lengths, a_gain, a_bias, f_gain, f_bias, b_up, b_down,
    inputs, cotangent, w_in_hbm, w_out_hbm, w_up_hbm, w_down_hbm,
    outs_hbm, backs_hbm, gathered, vectors, keep_probs,
    w_in, w_out, w_up, w_down, states, backs, bias, ones, spread, stat, inv, xhat, normal, normal_t, qkv, turned,
    probs, recip, mixed_t, hidden, total, scratch, wide, d_mixed, d_scores, d_query_t,
    grads, landed, landed_vectors,
    load_sem, save_sem, stash_sem, swap_send, swap_recv, sum_send, sum_recv, sum_local, sum_free,
):
    section = lax.axis_index("section")
    group = lax.axis_index("dp")
    micro = section // 2
    side = section % 2
    axes = {"x": Axis("section", section, 1), "y": Axis("section", section, 2), "core": Axis("dp", group, 1)}
    for i in range(bits):
        axes["z%d" % i] = Axis("dp", group, 2 << i)
    used = []

    def load(src, dst):
        copy = pltpu.make_async_copy(src, dst, load_sem.at[len(used)])
        copy.start()
        used.append(copy)
        return copy

    def load_attention(layer):
        return [load(w_in_hbm.at[layer], w_in), load(w_out_hbm.at[layer], w_out)]

    def load_feed(layer):
        return [load(w_up_hbm.at[layer], w_up), load(w_down_hbm.at[layer], w_down)]

    def wait(copies):
        for copy in copies:
            copy.wait()

    def stash(index, src, dst):
        copy = pltpu.make_async_copy(src, dst, stash_sem.at[index])
        copy.start()
        return copy

    first = [load(inputs.at[micro], states.at[0])]
    attention_loads = load_attention(0)

    barrier = pltpu.get_barrier_semaphore()
    for axis in axes.values():
        pl.semaphore_signal(barrier, inc=1, device_id=axis.device, device_id_type=MESH)
    build_mask(lengths, micro, bias)
    ones[...] = jnp.ones_like(ones)
    width = states.shape[2]
    row = lax.broadcasted_iota(jnp.int32, spread.shape, 0) * HEAD
    lane = lax.broadcasted_iota(jnp.int32, spread.shape, 1)
    spread[...] = jnp.where((lane >= row) & (lane < row + HEAD), 1.0, 0.0)
    vectors[...] = jnp.zeros_like(vectors)
    sums = Sums(grads, landed, gathered, vectors, landed_vectors, axes, side, (sum_send, sum_recv, sum_local, sum_free))
    partner = section + 2 - 4 * micro
    kept = []

    def swap(index, src, dst):
        return pltpu.make_async_remote_copy(
            src_ref=src.at[partner + 1 - index], dst_ref=dst.at[0, micro],
            send_sem=swap_send.at[index], recv_sem=swap_recv.at[index],
            device_id=axes["y"].device, device_id_type=MESH,
        )

    outward = swap(0, states, outs_hbm)

    def start_swap(copy, sublayer):
        @pl.when(partner == sublayer)
        def _():
            copy.start()

    def local(src, dst):
        copy = pltpu.make_async_copy(src, dst, save_sem.at[len(kept)])
        copy.start()
        kept.append(copy)

    def norm(sublayer):
        layer = sublayer // 2
        gain, shift = (a_gain, a_bias) if sublayer % 2 == 0 else (f_gain, f_bias)
        return (
            ones, gain[layer : layer + 1, :], shift[layer : layer + 1, :], stat, inv.at[sublayer], xhat.at[sublayer]
        )

    wait(first)
    saved = {}
    feed_loads, last = [], []

    def weights_here(layer):
        attention_loads[0].wait()
        if layer == 0:
            feed_loads.extend(load_feed(0))
            last.append(load(cotangent.at[micro], backs.at[4]))

    for layer in range(2):
        if layer == 1:
            saved["probs"].wait()
        attention_forward(
            functools.partial(weights_here, layer), attention_loads[1].wait,
            states.at[2 * layer], norm(2 * layer), w_in, w_out, bias, normal, qkv.at[layer], turned, probs,
            recip.at[layer], scratch, mixed_t.at[layer], states.at[2 * layer + 1],
        )
        if layer == 0:
            pl.semaphore_wait(barrier, len(axes))
        start_swap(outward, 2 * layer)
        if layer == 0:
            saved["probs"] = stash(0, probs, keep_probs)
            attention_loads = load_attention(1)
        wait(feed_loads)
        if layer == 1:
            break
        feed_forward(
            states.at[1], norm(1), w_up, b_up[:1, :], w_down, b_down[:1, :],
            normal, hidden, scratch, total, states.at[2],
        )
        start_swap(outward, 1)
        feed_loads = load_feed(1)
    swapped = 2 * states.shape[1] * width
    sums.now = 16.5
    sums.occupy("y", swapped // 2)
    sums.now = 20.5
    wait(last)
    seen = []

    def ready(layer):
        def start(at, size):
            for first in range(at, at + size, PIECE):
                task = len(seen)
                order, after, rank = ORDERS[task % len(ORDERS)]
                sums.begin(sums.block(layer, first, min(PIECE, at + size - first), order, after, task), rank)
                seen.append(first)

        return start

    def produced():
        start_swap(outward, 3)
        local(states.at[section + 1], outs_hbm.at[0, micro])

    for layer in (1, 0):
        if layer == 1:
            feed_both(
                states.at[3], backs.at[4], norm(3), w_up, b_up.at[1:2, :], w_down, b_down[1:2, :],
                normal, normal_t, hidden, wide, d_mixed, scratch, total, states.at[4], backs.at[3],
                grads.at[1], vectors.at[1], side, sums.tick, ready(1), produced,
            )
        else:
            wait(feed_loads)
            feed_both(
                states.at[1], backs.at[2], norm(1), w_up, b_up.at[:1, :], w_down, b_down[:1, :],
                normal, normal_t, hidden, wide, d_mixed, scratch, total, None, backs.at[1],
                grads.at[0], vectors.at[0], side, sums.tick, ready(0), None,
            )
        if layer == 1:
            feed_loads = load_feed(0)
        else:
            wait(attention_loads)
            saved["probs"].wait()
        attention_backward(
            backs.at[2 * layer + 1], norm(2 * layer), w_in, w_out, normal, normal_t, qkv.at[layer], turned, probs,
            recip.at[layer], scratch, mixed_t.at[layer], spread, d_mixed, d_scores, d_query_t,
            wide.at[:, : qkv.shape[2]], total, backs.at[2 * layer], grads.at[layer], vectors.at[layer],
            side, sums.tick, ready(layer),
        )
        sums.begin(sums.vector(layer), 0)
        if layer == 1:
            saved["probs"] = stash(1, keep_probs, probs)
            attention_loads = load_attention(0)
    def give(rows):
        push = Request(backs.at[partner, rows], backs_hbm.at[0, micro, rows], "y")
        yield [push]
        push.copy.wait_recv()

    local(backs.at[section], backs_hbm.at[0, micro])
    half = states.shape[1] // 2
    for at in (0, half):
        sums.begin(give(slice(at, at + half)), 1000)
    sums.drain()
    for copy in kept:
        copy.wait()
    outward.wait()


def run_chain(
    groups, inputs, cotangent, lengths, a_gain, a_bias, w_in, w_out, f_gain, f_bias, w_up, b_up, w_down, b_down
):
    _, count, width = inputs.shape
    layers, _, units = w_up.shape
    heads = width // HEAD
    bits = (groups // 2).bit_length() - 1
    vmem = pl.BlockSpec(memory_space=pltpu.VMEM)
    smem = pl.BlockSpec(memory_space=pltpu.SMEM)
    anywhere = pl.BlockSpec(memory_space=pl.ANY)
    shape = jax.ShapeDtypeStruct
    per_layer = 2 * width + units
    blocks = layers * (units // PIECE + 3)
    pushes = blocks * (3 * bits + 7) + layers * (bits + 2) + 2
    return pl.pallas_call(
        functools.partial(chain_kernel, bits),
        out_shape=(
            shape((1, 2, count, width), BF16),
            shape((1, 2, count, width), BF16),
            shape((2, layers, width, per_layer), BF16),
            shape((layers, 16, width), F32),
            shape((heads, count, count), BF16),
        ),
        in_specs=[smem] + [vmem] * 6 + [anywhere] * 6,
        out_specs=[anywhere] * 3 + [vmem] + [anywhere],
        scratch_shapes=[
            pltpu.VMEM(w_in.shape[1:], BF16),
            pltpu.VMEM(w_out.shape[1:], BF16),
            pltpu.VMEM(w_up.shape[1:], BF16),
            pltpu.VMEM(w_down.shape[1:], BF16),
            pltpu.VMEM((2 * layers + 1, count, width), BF16),
            pltpu.VMEM((2 * layers + 1, count, width), BF16),
            pltpu.VMEM((count, count), F32),
            pltpu.VMEM((width, LANES), BF16),
            pltpu.VMEM((heads, width), F32),
            pltpu.VMEM((2, count, LANES), F32),
            pltpu.VMEM((2 * layers, count, LANES), F32),
            pltpu.VMEM((2 * layers, count, width), BF16),
            pltpu.VMEM((count, width), BF16),
            pltpu.VMEM((width, count), BF16),
            pltpu.VMEM((layers, count, 3 * width), BF16),
            pltpu.VMEM((width, count), BF16),
            pltpu.VMEM((heads, count, count), BF16),
            pltpu.VMEM((layers, heads, 8, count), F32),
            pltpu.VMEM((layers, width, count), BF16),
            pltpu.VMEM((count, units), BF16),
            pltpu.VMEM((count, width), F32),
            pltpu.VMEM((2, count, CHUNK), F32),
            pltpu.VMEM((count, 3 * width), BF16),
            pltpu.VMEM((count, width), BF16),
            pltpu.VMEM((2, count, count), BF16),
            pltpu.VMEM((PAIR, count), F32),
            pltpu.VMEM((layers, width, per_layer), BF16),
            pltpu.VMEM((layers, width, per_layer), BF16),
            pltpu.VMEM((layers, bits + 2, 16, width), F32),
            pltpu.SemaphoreType.DMA((14,)),
            pltpu.SemaphoreType.DMA((2,)),
            pltpu.SemaphoreType.DMA((2,)),
            pltpu.SemaphoreType.DMA((2,)),
            pltpu.SemaphoreType.DMA((2,)),
            pltpu.SemaphoreType.DMA((pushes,)),
            pltpu.SemaphoreType.DMA((pushes,)),
            pltpu.SemaphoreType.DMA((2 * blocks,)),
            pltpu.SemaphoreType.REGULAR((3 * blocks,)),
        ],
        compiler_params=pltpu.CompilerParams(
            vmem_limit_bytes=63 * 1024 * 1024, collective_id=0, has_side_effects=True
        ),
        cost_estimate=pl.CostEstimate(
            flops=30_000_000_000, bytes_accessed=50_000_000, transcendentals=10_000_000
        ),
        name="chain",
    )(lengths[:, 0, :], a_gain, a_bias, f_gain, f_bias, b_up, b_down, inputs, cotangent, w_in, w_out, w_up, w_down)


def widen_kernel(
    block, vectors, outs_in, backs_in,
    g_in, g_out, g_up, g_down, a_gain, a_bias, f_gain, f_bias, b_up, b_down, outs, backs,
):
    width = g_out.shape[2]
    quarter = width // 2
    third = 3 * quarter
    units = g_up.shape[2] // 2
    parts = units // width
    first = (pl.program_id(0) == 0) & (pl.program_id(1) == 0)
    outs[...] = outs_in[...]
    backs[...] = backs_in[...]

    @pl.when(first)
    def _():
        for i, ref in enumerate([a_gain, a_bias, f_gain, f_bias, b_down]):
            ref[...] = vectors[:, i, :]
        for i in range(b_up.shape[1] // width):
            b_up[:, i * width : (i + 1) * width] = vectors[:, 5 + i, :]

    for side in range(2):
        for part in range(3):
            at = part * width + side * quarter
            g_in[0, :, at : at + quarter] = block[side, 0, :, part * quarter : (part + 1) * quarter].astype(F32)
        at = third
        g_out[0, :, side * quarter : (side + 1) * quarter] = block[side, 0, :, at : at + quarter].astype(F32)
        at += quarter
        g_up[0, :, side * units : (side + 1) * units] = block[side, 0, :, at : at + units].astype(F32)
        at += units
        for i in range(parts):
            g_down[0, side * parts + i] = block[side, 0, :, at + i * width : at + (i + 1) * width].astype(F32)


def widen(gathered, vectors, outs, backs):
    _, layers, width, cols = gathered.shape
    units = (cols - 2 * width) // 2
    parts = 2 * units // width
    shape = jax.ShapeDtypeStruct
    steps = width // WIDEN_ROWS
    stream = pl.BlockSpec((1, 1, outs.shape[2] // steps, width), lambda i, j: (0, i, j, 0))
    small = pl.BlockSpec((layers, width), lambda i, j: (0, 0))
    g_in, g_out, g_up, g_down, *rest = pl.pallas_call(
        widen_kernel,
        grid=(layers, steps),
        out_shape=(
            shape((layers, width, 3 * width), F32),
            shape((layers, width, width), F32),
            shape((layers, width, 2 * units), F32),
            shape((layers, parts, width, width), F32),
        )
        + (shape((layers, width), F32),) * 4
        + (shape((layers, 2 * units), F32), shape((layers, width), F32))
        + (shape(outs.shape, BF16), shape(backs.shape, BF16)),
        in_specs=[
            pl.BlockSpec((2, 1, WIDEN_ROWS, cols), lambda i, j: (0, i, j, 0)),
            pl.BlockSpec(vectors.shape, lambda i, j: (0, 0, 0)),
            stream,
            stream,
        ],
        out_specs=(
            pl.BlockSpec((1, WIDEN_ROWS, 3 * width), lambda i, j: (i, j, 0)),
            pl.BlockSpec((1, WIDEN_ROWS, width), lambda i, j: (i, j, 0)),
            pl.BlockSpec((1, WIDEN_ROWS, 2 * units), lambda i, j: (i, j, 0)),
            pl.BlockSpec((1, parts, WIDEN_ROWS, width), lambda i, j: (i, 0, j, 0)),
        )
        + (small,) * 4
        + (pl.BlockSpec((layers, 2 * units), lambda i, j: (0, 0)), small, stream, stream),
        compiler_params=pltpu.CompilerParams(vmem_limit_bytes=60 * 1024 * 1024),
        name="widen",
    )(gathered, vectors, outs, backs)
    return (g_in, g_out, g_up, g_down.reshape(layers, 2 * units, width), *rest)


def body(
    groups, inputs, cotangent, clip_lengths, attention_gain, attention_bias, attention_in, attention_out,
    feed_gain, feed_bias, feed_up, feed_up_bias, feed_down, feed_down_bias,
):
    outs, backs, gathered, vectors = run_chain(
        groups, inputs, cotangent, clip_lengths, attention_gain, attention_bias, attention_in, attention_out,
        feed_gain, feed_bias, feed_up, feed_up_bias, feed_down, feed_down_bias,
    )[:4]
    g_in, g_out, g_up, g_down, a_gain, a_bias, f_gain, f_bias, b_up, b_down, outs, backs = widen(
        gathered, vectors, outs, backs
    )
    return outs, backs, a_gain, a_bias, g_in, g_out, f_gain, f_bias, g_up, b_up, g_down, b_down


def solution(mesh):
    return jax.shard_map(
        functools.partial(body, mesh.shape["dp"]),
        mesh=mesh,
        in_specs=(P(None, "dp", None), P(None, "dp", None), P(None, "dp", None)) + (P(),) * 10,
        out_specs=(P("section", None, "dp", None), P("section", None, "dp", None)) + (P(),) * 10,
        check_vma=False,
    )
```
